512 devices in a mesh: orb: 128 (over x, z, core), aux: 4 (over y).
Axes of the slice: x: 4, y: 4, z: 16, core: 2. Of those that a mesh axis runs over, the one named last changes fastest.
Arguments:
- orbital_factors: bfloat16 [512, 384, 1536], P('orb', None, 'aux'), may hold values from -1 to 1
- metric_factor: bfloat16 [1536, 1536], P(None, 'aux'), may hold values from -0.15625 to 0.15625
- occ_energy: float32 [512], replicated, may hold values from -2 to -0.3
- vir_energy: float32 [384], replicated, may hold values from 0.2 to 3
- pair_list: int32 [768, 2], P('orb'), may hold values from 0 to 511, as said below
Outputs:
- gradient_factors: bfloat16 [512, 384, 1536], P('orb', None, 'aux')
The draws below stay inside these ranges and needn't reach their ends.
Inputs may be any that keep to these rules, and one draw needn't show every extreme that they name: `pair_list`: row r belongs to device r // 6 of orb, where orbital o is owned by device o // 4; its first entry is an orbital of that device; its second is an orbital of the device (r % 6) % 3 - 1 places further along orb, or of the row's own device where that place lies outside orb.
All inputs are finite; a program needn't handle non-finite values.
Results may differ from the reference program's by a relative error of at most 0.0083.
Values may be sent and summed in bfloat16 or wider, within the bound.
A program may use at most 64 MiB of HBM per device.

```python
import jax
import jax.numpy as jnp
from jax import lax

V = 384
NAUX = 1536
OCC_DEV = 4
PAIRS_DEV = 6
NOCC = 512


def draw_pair_list(key, part):
    owners = NOCC // OCC_DEV
    row_total = owners * PAIRS_DEV
    device = jnp.arange(row_total, dtype=jnp.int32) // PAIRS_DEV
    slot_ids = jnp.arange(row_total, dtype=jnp.int32) % PAIRS_DEV
    partner = jnp.clip(device + slot_ids % 3 - 1, 0, owners - 1)
    first_key, second_key = jax.random.split(jax.random.fold_in(key, 17))
    left_index = device * OCC_DEV + jax.random.randint(first_key, (row_total,), 0, OCC_DEV, dtype=jnp.int32)
    right_index = partner * OCC_DEV + jax.random.randint(second_key, (row_total,), 0, OCC_DEV, dtype=jnp.int32)
    return jnp.stack([left_index, right_index], axis=1).astype(jnp.int32)


def shard_levels(own_key, dims, cuts, least, high):
    gain = 1.0
    for dim, blocks in cuts:
        heights = jax.random.uniform(jax.random.fold_in(jax.random.fold_in(own_key, 6), dim), (blocks,), jnp.float32, least / len(cuts), high / len(cuts))
        gain = gain * jnp.repeat(jnp.exp(heights), dims[dim] // blocks).reshape((-1,) + (1,) * (len(dims) - 1 - dim))
    return gain


def scatter_about(own_key, dims, spread, most, cuts=(), kind=jnp.bfloat16):
    loudness = shard_levels(own_key, dims, cuts, -0.22, 0.18) if cuts else 1.0
    array = jax.random.normal(own_key, dims, jnp.float32) * spread * loudness
    return jnp.minimum(jnp.maximum(array, -most), most).astype(kind)


def setup_inputs(seed: int = 0) -> dict:
    key_of = jax.random.split(jax.random.key(seed), 6)
    orbital_factors = scatter_about(key_of[0], (NOCC, V, NAUX), 0.16, 1.0, ((0, 128), (2, 4)))
    metric_factor = scatter_about(key_of[1], (NAUX, NAUX), NAUX ** -0.5, 0.15625, ((1, 4),))
    occ_energy = jnp.clip(jax.random.uniform(key_of[2], (NOCC,), jnp.float32, -2.0, -0.3), -2.0, -0.3)
    vir_energy = jnp.clip(jax.random.uniform(key_of[3], (V,), jnp.float32, 0.2, 3.0), 0.2, 3.0)
    pair_list = draw_pair_list(jax.random.fold_in(key_of[5], 71), 0)
    return dict(orbital_factors=orbital_factors, metric_factor=metric_factor, occ_energy=occ_energy, vir_energy=vir_energy, pair_list=pair_list)


def reference(orbital_factors, metric_factor, occ_energy, vir_energy, pair_list):
    def add_pair(density_sum, pair_row):
        left_index = pair_row[0]
        right_index = pair_row[1]
        left_block = lax.dynamic_index_in_dim(orbital_factors, left_index, 0, keepdims=False)
        right_block = lax.dynamic_index_in_dim(orbital_factors, right_index, 0, keepdims=False)
        integrals = jnp.dot(left_block, right_block.T, preferred_element_type=jnp.float32)
        denominator = (occ_energy[left_index] + occ_energy[right_index]) - vir_energy[:, None] - vir_energy[None, :]
        amplitudes = (integrals / denominator).astype(jnp.bfloat16)
        left_term = jnp.dot(amplitudes, right_block, preferred_element_type=jnp.float32)
        right_term = jnp.dot(amplitudes.T, left_block, preferred_element_type=jnp.float32)
        density_sum = density_sum.at[left_index].add(left_term)
        density_sum = density_sum.at[right_index].add(right_term)
        return density_sum, None

    start_sum = jnp.zeros(orbital_factors.shape, jnp.float32)
    density_sum, unused = lax.scan(add_pair, start_sum, pair_list)
    density = density_sum.astype(jnp.bfloat16)
    flat = density.reshape(-1, NAUX)
    result = jnp.dot(flat, metric_factor, preferred_element_type=jnp.float32)
    return result.astype(jnp.bfloat16).reshape(NOCC, V, NAUX)
```

```python
import functools

import jax
import jax.numpy as jnp
from jax import lax
from jax.experimental import pallas as pl
from jax.experimental.pallas import tpu as pltpu
from jax.sharding import PartitionSpec as P

MESH = pl.DeviceIdType.MESH
F32 = jnp.float32
BF16 = jnp.bfloat16
CHUNKS = 4


def dot(a, b):
    return lax.dot_general(a, b, (((1,), (0,)), ((), ())), preferred_element_type=F32)


def dot_nt(a, b):
    return lax.dot_general(a, b, (((1,), (1,)), ((), ())), preferred_element_type=F32)


def dot_tn(a, b):
    return lax.dot_general(a, b, (((0,), (0,)), ((), ())), preferred_element_type=F32)


def kernel(
    n_orb,
    b_hbm,
    m_hbm,
    occ,
    vir,
    pairs,
    out,
    bown,
    m,
    gathered,
    halo_l,
    halo_r,
    stage_l,
    stage_r,
    got_l,
    got_r,
    ids,
    acc_i,
    recip,
    acc_c,
    cb,
    amp,
    term,
    total,
    tsend_l,
    tsend_r,
    trecv_l,
    trecv_r,
    load_sem,
    id_send,
    id_recv,
    y_send,
    y_recv,
    z_send,
    z_recv,
    t_send,
    t_recv,
):
    owned, virt, width = bown.shape
    rows = virt // CHUNKS
    half = CHUNKS // 2
    o = lax.axis_index("orb")
    y = lax.axis_index("aux")
    has_l = o > 0
    has_r = o < n_orb - 1
    up, down = lax.rem(y + 1, 4), lax.rem(y + 3, 4)
    to_up, to_down = (o, up), (o, down)
    to_l, to_r = (o - 1, y), (o + 1, y)

    load_b = pltpu.make_async_copy(b_hbm, bown, load_sem.at[0])
    load_m = pltpu.make_async_copy(m_hbm, m, load_sem.at[1])
    load_b.start()
    load_m.start()

    barrier = pltpu.get_barrier_semaphore()
    pl.semaphore_signal(barrier, inc=1, device_id=to_up, device_id_type=MESH)
    pl.semaphore_signal(barrier, inc=1, device_id=to_down, device_id_type=MESH)

    @pl.when(has_l)
    def _():
        pl.semaphore_signal(barrier, inc=1, device_id=to_l, device_id_type=MESH)

    @pl.when(has_r)
    def _():
        pl.semaphore_signal(barrier, inc=1, device_id=to_r, device_id_type=MESH)

    pl.semaphore_wait(barrier, 2 + has_l.astype(jnp.int32) + has_r.astype(jnp.int32))
    load_b.wait()

    def remote(src, dst, send, recv, device):
        return pltpu.make_async_remote_copy(
            src_ref=src, dst_ref=dst, send_sem=send, recv_sem=recv, device_id=device, device_id_type=MESH
        )

    ids_l = remote(pairs, got_r, id_send.at[0], id_recv.at[0], to_l)
    ids_r = remote(pairs, got_l, id_send.at[1], id_recv.at[1], to_r)

    @pl.when(has_l)
    def _():
        ids_l.start()

    @pl.when(has_r)
    def _():
        ids_r.start()

    def row_span(c):
        return pl.ds(c * rows, rows)

    send_up = [
        remote(bown.at[:, row_span(c)], gathered[0][c], y_send.at[0, c], y_recv.at[0, c], to_up) for c in range(CHUNKS)
    ]
    send_down = [
        remote(bown.at[:, row_span(c)], gathered[1][c], y_send.at[1, c], y_recv.at[1, c], to_down) for c in range(CHUNKS)
    ]
    pass_on = [
        remote(gathered[0][c], gathered[2][c], y_send.at[2, c], y_recv.at[2, c], to_up)
        if c < half
        else remote(gathered[1][c], gathered[2][c], y_send.at[2, c], y_recv.at[2, c], to_down)
        for c in range(CHUNKS)
    ]
    up_order = list(range(CHUNKS))
    down_order = up_order[half:] + up_order[:half]
    for cu, cd in zip(up_order, down_order):
        send_up[cu].start()
        send_down[cd].start()

    @pl.when(has_l)
    def _():
        ids_r.wait_recv()
        for q in range(2):
            ids[q] = lax.rem(got_l[3 * q + 2, 1], owned)

    @pl.when(jnp.logical_not(has_l))
    def _():
        for q in range(2):
            ids[q] = lax.rem(pairs[3 * q, 1], owned)

    @pl.when(has_r)
    def _():
        ids_l.wait_recv()
        for q in range(2):
            ids[2 + q] = lax.rem(got_r[3 * q, 1], owned)

    @pl.when(jnp.logical_not(has_r))
    def _():
        for q in range(2):
            ids[2 + q] = lax.rem(pairs[3 * q + 2, 1], owned)

    def halo_left(s, c):
        span = row_span(c)
        return remote(stage_l.at[s, :, span], halo_r.at[s, :, span], z_send.at[0, s, c], z_recv.at[0, s, c], to_l)

    def halo_right(s, c):
        span = row_span(c)
        return remote(stage_r.at[s, :, span], halo_l.at[s, :, span], z_send.at[1, s, c], z_recv.at[1, s, c], to_r)

    def pick(s, c, k):
        return bown[k, row_span(c), :] if s == 0 else gathered[s - 1][c][k]

    def stage(s, c):
        span = row_span(c)

        @pl.when(has_l)
        def _():
            for q in range(2):
                stage_l[s, q, span, :] = pick(s, c, ids[q])
            halo_left(s, c).start()

        @pl.when(jnp.logical_not(has_l))
        def _():
            for q in range(2):
                halo_l[s, q, span, :] = pick(s, c, ids[q])

        @pl.when(has_r)
        def _():
            for q in range(2):
                stage_r[s, q, span, :] = pick(s, c, ids[2 + q])
            halo_right(s, c).start()

        @pl.when(jnp.logical_not(has_r))
        def _():
            for q in range(2):
                halo_r[s, q, span, :] = pick(s, c, ids[2 + q])

    def halo_wait(s):
        for c in range(CHUNKS):
            @pl.when(has_r)
            def _():
                halo_left(s, c).wait_recv()

            @pl.when(has_l)
            def _():
                halo_right(s, c).wait_recv()

    def own(s, k):
        return bown[k] if s == 0 else jnp.concatenate([g[k] for g in gathered[s - 1]], axis=0)

    def metric_rows(s):
        source = lax.rem(y + (0, 3, 1, 2)[s], 4)
        return m[pl.ds(pl.multiple_of(source * width, width), width), :]

    def put_c(s, slot, value):
        if s == 0:
            acc_c[slot] = value
        elif s < 3:
            acc_c[slot] += value
        else:
            cb[slot] = (acc_c[slot] + value).astype(BF16)

    def put_i(s, slot, value):
        if s == 0:
            acc_i[slot] = value
        elif s < 3:
            acc_i[slot] += value
        else:
            amp[slot] = ((acc_i[slot] + value) * recip[slot]).astype(BF16)

    def compute_own(s):
        @pl.loop(0, owned)
        def _(k):
            put_c(s, k, dot(own(s, k), metric_rows(s)))

        @pl.loop(0, 2)
        def _(q):
            p = 3 * q + 1
            put_i(s, p, dot_nt(own(s, lax.rem(pairs[p, 0], owned)), own(s, lax.rem(pairs[p, 1], owned))))

    def compute_halo(s):
        @pl.loop(0, 2)
        def _(q):
            p = 3 * q
            put_i(s, p, dot_nt(own(s, lax.rem(pairs[p, 0], owned)), halo_l[s, q]))
            put_i(s, p + 2, dot_nt(own(s, lax.rem(pairs[p + 2, 0], owned)), halo_r[s, q]))

    def compute_halo_c(s):
        @pl.loop(0, 2)
        def _(q):
            put_c(s, owned + q, dot(halo_l[s, q], metric_rows(s)))
            put_c(s, owned + 2 + q, dot(halo_r[s, q], metric_rows(s)))

    for c in range(CHUNKS):
        stage(0, c)

    lanes = min(128, virt)
    vir_rows = jnp.broadcast_to(vir[...], (lanes, virt))
    vir_cols = vir_rows.T

    @pl.loop(0, 6)
    def _(p):
        energy = occ[pairs[p, 0]] + occ[pairs[p, 1]]
        for t in range(virt // lanes):
            span = slice(t * lanes, (t + 1) * lanes)
            recip[p, :, span] = 1.0 / ((energy - vir_cols) - vir[:, span])

    load_m.wait()
    compute_own(0)

    for cu, cd in zip(up_order, down_order):
        send_up[cu].wait_recv()
        if cu < half:
            pass_on[cu].start()
        stage(1, cu)
        send_down[cd].wait_recv()
        if cd >= half:
            pass_on[cd].start()
        stage(2, cd)

    halo_wait(0)
    compute_halo(0)
    compute_halo_c(0)
    for s in (1, 2):
        compute_own(s)
        halo_wait(s)
        compute_halo(s)
        compute_halo_c(s)

    for c in range(half):
        for d in (c, half + c):
            pass_on[d].wait_recv()
            stage(3, d)
    compute_own(3)
    halo_wait(3)
    compute_halo(3)

    term_l = [remote(tsend_l.at[q], trecv_r.at[q], t_send.at[0, q], t_recv.at[0, q], to_l) for q in range(2)]
    term_r = [remote(tsend_r.at[q], trecv_l.at[q], t_send.at[1, q], t_recv.at[1, q], to_r) for q in range(2)]
    for q in range(2):
        for side, p, has, copy, far, near in (
            (0, 3 * q, has_l, term_l[q], tsend_l, trecv_l),
            (1, 3 * q + 2, has_r, term_r[q], tsend_r, trecv_r),
        ):
            value = dot_tn(amp[p], cb[lax.rem(pairs[p, 0], owned)]).astype(BF16)

            @pl.when(has)
            def _():
                far[q] = value
                copy.start()

            @pl.when(jnp.logical_not(has))
            def _():
                near[q] = value

    compute_halo_c(3)

    @pl.loop(0, 2)
    def _(q):
        p = 3 * q
        term[p] = dot(amp[p], cb[owned + q])
        term[p + 1] = dot(amp[p + 1], cb[lax.rem(pairs[p + 1, 1], owned)])
        term[p + 2] = dot(amp[p + 2], cb[owned + 2 + q])
        term[6 + q] = dot_tn(amp[p + 1], cb[lax.rem(pairs[p + 1, 0], owned)])

    step = 16
    targets = [lax.rem(pairs[p, 0], owned) for p in range(6)] + [lax.rem(pairs[3 * q + 1, 1], owned) for q in range(2)]

    @pl.loop(0, virt // step)
    def _(t):
        span = pl.ds(pl.multiple_of(t * step, step), step)
        values = [term[n, span, :] for n in range(8)]
        for k in range(owned):
            total[k, span, :] = sum(jnp.where(target == k, 1.0, 0.0) * v for target, v in zip(targets, values))

    for q in range(2):

        @pl.when(has_r)
        def _():
            term_l[q].wait_recv()

        @pl.when(has_l)
        def _():
            term_r[q].wait_recv()

    arrived = [ids[n] for n in range(4)]

    @pl.loop(0, virt // step)
    def _(t):
        span = pl.ds(pl.multiple_of(t * step, step), step)
        values = [trecv_l[q, span, :].astype(F32) for q in range(2)] + [trecv_r[q, span, :].astype(F32) for q in range(2)]
        for k in range(owned):
            more = sum(jnp.where(target == k, 1.0, 0.0) * v for target, v in zip(arrived, values))
            out[k, span, :] = (total[k, span, :] + more).astype(BF16)

    for c in range(CHUNKS):
        send_up[c].wait_send()
        send_down[c].wait_send()
        pass_on[c].wait_send()

    @pl.when(has_l)
    def _():
        ids_l.wait_send()
        for q in range(2):
            term_l[q].wait_send()
        for s in range(4):
            for c in range(CHUNKS):
                halo_left(s, c).wait_send()

    @pl.when(has_r)
    def _():
        ids_r.wait_send()
        for q in range(2):
            term_r[q].wait_send()
        for s in range(4):
            for c in range(CHUNKS):
                halo_right(s, c).wait_send()


def local(n_orb, b, metric, occ, vir, pairs):
    owned, virt, width = b.shape
    rows = virt // CHUNKS
    vmem = pltpu.VMEM
    dma = pltpu.SemaphoreType.DMA
    scratch = [
        vmem((owned, virt, width), BF16),
        vmem(metric.shape, BF16),
        tuple(tuple(vmem((owned, rows, width), BF16) for _ in range(CHUNKS)) for _ in range(3)),
        vmem((4, 2, virt, width), BF16),
        vmem((4, 2, virt, width), BF16),
        vmem((4, 2, virt, width), BF16),
        vmem((4, 2, virt, width), BF16),
        pltpu.SMEM(pairs.shape, jnp.int32),
        pltpu.SMEM(pairs.shape, jnp.int32),
        pltpu.SMEM((4,), jnp.int32),
        vmem((6, virt, virt), F32),
        vmem((6, virt, virt), F32),
        vmem((owned + 4, virt, width), F32),
        vmem((owned + 4, virt, width), BF16),
        vmem((6, virt, virt), BF16),
        vmem((8, virt, width), F32),
        vmem((owned, virt, width), F32),
        vmem((2, virt, width), BF16),
        vmem((2, virt, width), BF16),
        vmem((2, virt, width), BF16),
        vmem((2, virt, width), BF16),
        dma((2,)),
        dma((2,)),
        dma((2,)),
        dma((3, CHUNKS)),
        dma((3, CHUNKS)),
        dma((2, 4, CHUNKS)),
        dma((2, 4, CHUNKS)),
        dma((2, 2)),
        dma((2, 2)),
    ]
    return pl.pallas_call(
        functools.partial(kernel, n_orb),
        out_shape=jax.ShapeDtypeStruct(b.shape, BF16),
        in_specs=[
            pl.BlockSpec(memory_space=pl.ANY),
            pl.BlockSpec(memory_space=pl.ANY),
            pl.BlockSpec(memory_space=pltpu.SMEM),
            pl.BlockSpec(memory_space=pltpu.VMEM),
            pl.BlockSpec(memory_space=pltpu.SMEM),
        ],
        out_specs=pl.BlockSpec(memory_space=pltpu.VMEM),
        scratch_shapes=scratch,
        compiler_params=pltpu.CompilerParams(
            collective_id=0, has_side_effects=True, vmem_limit_bytes=52 * 2**20
        ),
    )(b, metric, occ, vir.reshape(1, -1), pairs)


def solution(mesh):
    placed = (P("orb", None, "aux"), P(None, "aux"), P(), P(), P("orb", None))
    return jax.shard_map(
        functools.partial(local, mesh.shape["orb"]),
        mesh=mesh,
        in_specs=placed,
        out_specs=P("orb", None, "aux"),
        check_vma=False,
    )
```

```python
import functools

import jax
import jax.numpy as jnp
from jax import lax
from jax.experimental import pallas as pl
from jax.experimental.pallas import tpu as pltpu
from jax.sharding import PartitionSpec as P

MESH = pl.DeviceIdType.MESH
F32 = jnp.float32
BF16 = jnp.bfloat16
CHUNKS = 4


def dot(a, b):
    return lax.dot_general(a, b, (((1,), (0,)), ((), ())), preferred_element_type=F32)


def dot_nt(a, b):
    return lax.dot_general(a, b, (((1,), (1,)), ((), ())), preferred_element_type=F32)


def dot_tn(a, b):
    return lax.dot_general(a, b, (((0,), (0,)), ((), ())), preferred_element_type=F32)


def kernel(
    n_orb,
    b_hbm,
    m_hbm,
    occ_hbm,
    vir_hbm,
    pairs_hbm,
    out,
    occ,
    vir,
    pairs,
    bown,
    m,
    gathered,
    halo_l,
    halo_r,
    stage_l,
    stage_r,
    got_l,
    got_r,
    ids,
    acc_i,
    recip,
    acc_c,
    cb,
    amp,
    term,
    total,
    tsend_l,
    tsend_r,
    trecv_l,
    trecv_r,
    load_sem,
    entered,
    id_send,
    id_recv,
    y_send,
    y_recv,
    z_send,
    z_recv,
    t_send,
    t_recv,
):
    owned, virt, width = bown.shape
    rows = virt // CHUNKS
    half = CHUNKS // 2
    o = lax.axis_index("orb")
    y = lax.axis_index("aux")
    has_l = o > 0
    has_r = o < n_orb - 1
    up, down = lax.rem(y + 1, 4), lax.rem(y + 3, 4)
    to_up, to_down = (o, up), (o, down)
    to_l, to_r = (o - 1, y), (o + 1, y)

    load_b = pltpu.make_async_copy(b_hbm, bown, load_sem.at[0])
    load_m = pltpu.make_async_copy(m_hbm, m, load_sem.at[1])
    load_pairs = pltpu.make_async_copy(pairs_hbm, pairs, load_sem.at[2])
    load_occ = pltpu.make_async_copy(occ_hbm, occ, load_sem.at[3])
    load_vir = pltpu.make_async_copy(vir_hbm, vir, load_sem.at[4])
    load_pairs.start()
    load_b.start()
    load_occ.start()
    load_vir.start()
    load_m.start()

    barrier = pltpu.get_barrier_semaphore()
    pl.semaphore_signal(barrier, inc=1, device_id=to_up, device_id_type=MESH)
    pl.semaphore_signal(barrier, inc=1, device_id=to_down, device_id_type=MESH)

    @pl.when(has_l)
    def _():
        pl.semaphore_signal(barrier, inc=1, device_id=to_l, device_id_type=MESH)

    pl.semaphore_wait(barrier, 2 + has_r.astype(jnp.int32))

    @pl.when(has_r)
    def _():
        pl.semaphore_signal(entered, inc=1, device_id=to_r, device_id_type=MESH)

    load_pairs.wait()
    load_b.wait()

    def remote(src, dst, send, recv, device):
        return pltpu.make_async_remote_copy(
            src_ref=src, dst_ref=dst, send_sem=send, recv_sem=recv, device_id=device, device_id_type=MESH
        )

    ids_l = remote(pairs, got_r, id_send.at[0], id_recv.at[0], to_l)
    ids_r = remote(pairs, got_l, id_send.at[1], id_recv.at[1], to_r)

    def row_span(c):
        return pl.ds(c * rows, rows)

    send_up = [
        remote(bown.at[:, row_span(c)], gathered[0][c], y_send.at[0, c], y_recv.at[0, c], to_up) for c in range(CHUNKS)
    ]
    send_down = [
        remote(bown.at[:, row_span(c)], gathered[1][c], y_send.at[1, c], y_recv.at[1, c], to_down) for c in range(CHUNKS)
    ]
    pass_on = [
        remote(gathered[0][c], gathered[2][c], y_send.at[2, c], y_recv.at[2, c], to_up)
        if c < half
        else remote(gathered[1][c], gathered[2][c], y_send.at[2, c], y_recv.at[2, c], to_down)
        for c in range(CHUNKS)
    ]
    up_order = list(range(CHUNKS))
    down_order = up_order[half:] + up_order[:half]
    for cu, cd in zip(up_order, down_order):
        send_up[cu].start()
        send_down[cd].start()

    @pl.when(has_r)
    def _():
        ids_r.start()

    @pl.when(has_l)
    def _():
        pl.semaphore_wait(entered, 1)
        ids_l.start()

    @pl.when(has_l)
    def _():
        ids_r.wait_recv()
        for q in range(2):
            ids[q] = lax.rem(got_l[1, 3 * q + 2], owned)

    @pl.when(jnp.logical_not(has_l))
    def _():
        for q in range(2):
            ids[q] = lax.rem(pairs[1, 3 * q], owned)

    @pl.when(has_r)
    def _():
        ids_l.wait_recv()
        for q in range(2):
            ids[2 + q] = lax.rem(got_r[1, 3 * q], owned)

    @pl.when(jnp.logical_not(has_r))
    def _():
        for q in range(2):
            ids[2 + q] = lax.rem(pairs[1, 3 * q + 2], owned)

    def halo_left(s, c):
        span = row_span(c)
        return remote(stage_l.at[s, :, span], halo_r.at[s, :, span], z_send.at[0, s, c], z_recv.at[0, s, c], to_l)

    def halo_right(s, c):
        span = row_span(c)
        return remote(stage_r.at[s, :, span], halo_l.at[s, :, span], z_send.at[1, s, c], z_recv.at[1, s, c], to_r)

    def pick(s, c, k):
        return bown[k, row_span(c), :] if s == 0 else gathered[s - 1][c][k]

    def stage(s, c):
        span = row_span(c)

        @pl.when(has_l)
        def _():
            for q in range(2):
                stage_l[s, q, span, :] = pick(s, c, ids[q])
            halo_left(s, c).start()

        @pl.when(jnp.logical_not(has_l))
        def _():
            for q in range(2):
                halo_l[s, q, span, :] = pick(s, c, ids[q])

        @pl.when(has_r)
        def _():
            for q in range(2):
                stage_r[s, q, span, :] = pick(s, c, ids[2 + q])
            halo_right(s, c).start()

        @pl.when(jnp.logical_not(has_r))
        def _():
            for q in range(2):
                halo_r[s, q, span, :] = pick(s, c, ids[2 + q])

    def wait_right(s):
        @pl.when(has_r)
        def _():
            for c in range(CHUNKS):
                halo_left(s, c).wait_recv()

    def wait_left(s):
        @pl.when(has_l)
        def _():
            for c in range(CHUNKS):
                halo_right(s, c).wait_recv()

    def halo_wait(s):
        wait_right(s)
        wait_left(s)

    def own(s, k):
        return bown[k] if s == 0 else jnp.concatenate([g[k] for g in gathered[s - 1]], axis=0)

    def metric_rows(s):
        source = lax.rem(y + (0, 3, 1, 2)[s], 4)
        return m[pl.ds(pl.multiple_of(source * width, width), width), :]

    def put_c(s, slot, value):
        if s == 0:
            acc_c[slot] = value
        elif s < 3:
            acc_c[slot] += value
        else:
            cb[slot] = (acc_c[slot] + value).astype(BF16)

    def put_i(s, slot, value):
        if s == 0:
            acc_i[slot] = value
        elif s < 3:
            acc_i[slot] += value
        else:
            amp[slot] = ((acc_i[slot] + value) * recip[slot]).astype(BF16)

    def compute_own(s):
        @pl.loop(0, owned)
        def _(k):
            put_c(s, k, dot(own(s, k), metric_rows(s)))

        @pl.loop(0, 2)
        def _(q):
            p = 3 * q + 1
            put_i(s, p, dot_nt(own(s, lax.rem(pairs[0, p], owned)), own(s, lax.rem(pairs[1, p], owned))))

    def compute_left(s, q):
        put_i(s, 3 * q, dot_nt(own(s, lax.rem(pairs[0, 3 * q], owned)), halo_l[s, q]))

    def compute_right(s, q):
        put_i(s, 3 * q + 2, dot_nt(own(s, lax.rem(pairs[0, 3 * q + 2], owned)), halo_r[s, q]))

    def compute_halo(s):
        @pl.loop(0, 2)
        def _(q):
            compute_left(s, q)
            compute_right(s, q)

    def compute_halo_c(s):
        @pl.loop(0, 2)
        def _(q):
            put_c(s, owned + q, dot(halo_l[s, q], metric_rows(s)))
            put_c(s, owned + 2 + q, dot(halo_r[s, q], metric_rows(s)))

    for c in range(CHUNKS):
        stage(0, c)

    lanes = min(128, virt)
    load_occ.wait()
    load_vir.wait()
    vir_row = vir[...].reshape(1, virt)
    vir_rows = jnp.broadcast_to(vir_row, (lanes, virt))
    vir_cols = vir_rows.T

    @pl.loop(0, 6)
    def _(p):
        energy = occ[pairs[0, p]] + occ[pairs[1, p]]
        for t in range(virt // lanes):
            span = slice(t * lanes, (t + 1) * lanes)
            recip[p, :, span] = 1.0 / ((energy - vir_cols) - vir_row[:, span])

    load_m.wait()
    compute_own(0)

    for cu, cd in zip(up_order, down_order):
        send_up[cu].wait_recv()
        if cu < half:
            pass_on[cu].start()
        stage(1, cu)
        send_down[cd].wait_recv()
        if cd >= half:
            pass_on[cd].start()
        stage(2, cd)

    halo_wait(0)
    compute_halo(0)
    compute_halo_c(0)
    for s in (1, 2):
        compute_own(s)
        halo_wait(s)
        compute_halo(s)
        compute_halo_c(s)

    for c in range(half):
        for d in (c, half + c):
            pass_on[d].wait_recv()
            stage(3, d)
    compute_own(3)
    term_l = [remote(tsend_l.at[q], trecv_r.at[q], t_send.at[0, q], t_recv.at[0, q], to_l) for q in range(2)]
    term_r = [remote(tsend_r.at[q], trecv_l.at[q], t_send.at[1, q], t_recv.at[1, q], to_r) for q in range(2)]
    for ready, work, slot, has, copies, far, near in (
        (wait_right, compute_right, 2, has_r, term_r, tsend_r, trecv_r),
        (wait_left, compute_left, 0, has_l, term_l, tsend_l, trecv_l),
    ):
        ready(3)
        for q in range(2):
            p = 3 * q + slot
            work(3, q)
            value = dot_tn(amp[p], cb[lax.rem(pairs[0, p], owned)]).astype(BF16)

            @pl.when(has)
            def _():
                far[q] = value
                copies[q].start()

            @pl.when(jnp.logical_not(has))
            def _():
                near[q] = value

    compute_halo_c(3)

    @pl.loop(0, 2)
    def _(q):
        p = 3 * q
        term[p] = dot(amp[p], cb[owned + q])
        term[p + 1] = dot(amp[p + 1], cb[lax.rem(pairs[1, p + 1], owned)])
        term[p + 2] = dot(amp[p + 2], cb[owned + 2 + q])
        term[6 + q] = dot_tn(amp[p + 1], cb[lax.rem(pairs[0, p + 1], owned)])

    step = 16
    targets = [lax.rem(pairs[0, p], owned) for p in range(6)] + [lax.rem(pairs[1, 3 * q + 1], owned) for q in range(2)]

    @pl.loop(0, virt // step)
    def _(t):
        span = pl.ds(pl.multiple_of(t * step, step), step)
        values = [term[n, span, :] for n in range(8)]
        for k in range(owned):
            total[k, span, :] = sum(jnp.where(target == k, 1.0, 0.0) * v for target, v in zip(targets, values))

    for q in range(2):

        @pl.when(has_r)
        def _():
            term_l[q].wait_recv()

        @pl.when(has_l)
        def _():
            term_r[q].wait_recv()

    arrived = [ids[n] for n in range(4)]

    @pl.loop(0, virt // step)
    def _(t):
        span = pl.ds(pl.multiple_of(t * step, step), step)
        values = [trecv_l[q, span, :].astype(F32) for q in range(2)] + [trecv_r[q, span, :].astype(F32) for q in range(2)]
        for k in range(owned):
            more = sum(jnp.where(target == k, 1.0, 0.0) * v for target, v in zip(arrived, values))
            out[k, span, :] = (total[k, span, :] + more).astype(BF16)

    for c in range(CHUNKS):
        send_up[c].wait_send()
        send_down[c].wait_send()
        pass_on[c].wait_send()

    @pl.when(has_l)
    def _():
        ids_l.wait_send()
        for q in range(2):
            term_l[q].wait_send()
        for s in range(4):
            for c in range(CHUNKS):
                halo_left(s, c).wait_send()

    @pl.when(has_r)
    def _():
        ids_r.wait_send()
        for q in range(2):
            term_r[q].wait_send()
        for s in range(4):
            for c in range(CHUNKS):
                halo_right(s, c).wait_send()


def local(n_orb, b, metric, occ, vir, pairs):
    pairs_t = pairs.T
    owned, virt, width = b.shape
    rows = virt // CHUNKS
    vmem = pltpu.VMEM
    dma = pltpu.SemaphoreType.DMA
    scratch = [
        pltpu.SMEM(occ.shape, F32),
        vmem(vir.shape, F32),
        pltpu.SMEM(pairs_t.shape, jnp.int32),
        vmem((owned, virt, width), BF16),
        vmem(metric.shape, BF16),
        tuple(tuple(vmem((owned, rows, width), BF16) for _ in range(CHUNKS)) for _ in range(3)),
        vmem((4, 2, virt, width), BF16),
        vmem((4, 2, virt, width), BF16),
        vmem((4, 2, virt, width), BF16),
        vmem((4, 2, virt, width), BF16),
        pltpu.SMEM(pairs_t.shape, jnp.int32),
        pltpu.SMEM(pairs_t.shape, jnp.int32),
        pltpu.SMEM((4,), jnp.int32),
        vmem((6, virt, virt), F32),
        vmem((6, virt, virt), F32),
        vmem((owned + 4, virt, width), F32),
        vmem((owned + 4, virt, width), BF16),
        vmem((6, virt, virt), BF16),
        vmem((8, virt, width), F32),
        vmem((owned, virt, width), F32),
        vmem((2, virt, width), BF16),
        vmem((2, virt, width), BF16),
        vmem((2, virt, width), BF16),
        vmem((2, virt, width), BF16),
        dma((5,)),
        pltpu.SemaphoreType.REGULAR,
        dma((2,)),
        dma((2,)),
        dma((3, CHUNKS)),
        dma((3, CHUNKS)),
        dma((2, 4, CHUNKS)),
        dma((2, 4, CHUNKS)),
        dma((2, 2)),
        dma((2, 2)),
    ]
    return pl.pallas_call(
        functools.partial(kernel, n_orb),
        out_shape=jax.ShapeDtypeStruct(b.shape, BF16),
        in_specs=[pl.BlockSpec(memory_space=pltpu.HBM)] * 5,
        out_specs=pl.BlockSpec(memory_space=pltpu.VMEM),
        scratch_shapes=scratch,
        compiler_params=pltpu.CompilerParams(
            collective_id=0, has_side_effects=True, vmem_limit_bytes=52 * 2**20
        ),
    )(b, metric, occ, vir, pairs_t)


def solution(mesh):
    placed = (P("orb", None, "aux"), P(None, "aux"), P(), P(), P("orb", None))
    return jax.shard_map(
        functools.partial(local, mesh.shape["orb"]),
        mesh=mesh,
        in_specs=placed,
        out_specs=P("orb", None, "aux"),
        check_vma=False,
    )
```

```python
import functools

import jax
import jax.numpy as jnp
from jax import lax
from jax.experimental import pallas as pl
from jax.experimental.pallas import tpu as pltpu
from jax.sharding import PartitionSpec as P

MESH = pl.DeviceIdType.MESH
F32 = jnp.float32
BF16 = jnp.bfloat16
CHUNKS = 4


def dot(a, b):
    return lax.dot_general(a, b, (((1,), (0,)), ((), ())), preferred_element_type=F32)


def dot_nt(a, b):
    return lax.dot_general(a, b, (((1,), (1,)), ((), ())), preferred_element_type=F32)


def dot_tn(a, b):
    return lax.dot_general(a, b, (((0,), (0,)), ((), ())), preferred_element_type=F32)


def kernel(
    n_orb,
    b_hbm,
    m_hbm,
    occ_hbm,
    vir_hbm,
    pairs_hbm,
    out,
    occ,
    vir,
    pairs,
    bown,
    m,
    gathered,
    halo_l,
    halo_r,
    stage_l,
    stage_r,
    got_l,
    got_r,
    ids,
    acc_i,
    recip,
    acc_c,
    cb,
    amp,
    term,
    total,
    tsend_l,
    tsend_r,
    trecv_l,
    trecv_r,
    load_sem,
    entered,
    id_send,
    id_recv,
    y_send,
    y_recv,
    z_send,
    z_recv,
    t_send,
    t_recv,
):
    owned, virt, width = bown.shape
    rows = virt // CHUNKS
    half = CHUNKS // 2
    o = lax.axis_index("orb")
    y = lax.axis_index("aux")
    has_l = o > 0
    has_r = o < n_orb - 1
    up, down = lax.rem(y + 1, 4), lax.rem(y + 3, 4)
    to_up, to_down = (o, up), (o, down)
    to_l, to_r = (o - 1, y), (o + 1, y)

    load_b = pltpu.make_async_copy(b_hbm, bown, load_sem.at[0])
    load_m = pltpu.make_async_copy(m_hbm, m, load_sem.at[1])
    load_pairs = pltpu.make_async_copy(pairs_hbm, pairs, load_sem.at[2])
    load_occ = pltpu.make_async_copy(occ_hbm, occ, load_sem.at[3])
    load_vir = pltpu.make_async_copy(vir_hbm, vir, load_sem.at[4])
    load_pairs.start()
    load_b.start()
    load_occ.start()
    load_vir.start()
    load_m.start()

    barrier = pltpu.get_barrier_semaphore()
    pl.semaphore_signal(barrier, inc=1, device_id=to_up, device_id_type=MESH)
    pl.semaphore_signal(barrier, inc=1, device_id=to_down, device_id_type=MESH)

    @pl.when(has_l)
    def _():
        pl.semaphore_signal(barrier, inc=1, device_id=to_l, device_id_type=MESH)

    pl.semaphore_wait(barrier, 2 + has_r.astype(jnp.int32))

    @pl.when(has_r)
    def _():
        pl.semaphore_signal(entered, inc=1, device_id=to_r, device_id_type=MESH)

    load_pairs.wait()
    load_b.wait()

    def remote(src, dst, send, recv, device):
        return pltpu.make_async_remote_copy(
            src_ref=src, dst_ref=dst, send_sem=send, recv_sem=recv, device_id=device, device_id_type=MESH
        )

    ids_l = remote(pairs, got_r, id_send.at[0], id_recv.at[0], to_l)
    ids_r = remote(pairs, got_l, id_send.at[1], id_recv.at[1], to_r)

    def row_span(c):
        return pl.ds(c * rows, rows)

    send_up = [
        remote(bown.at[:, row_span(c)], gathered[0][c], y_send.at[0, c], y_recv.at[0, c], to_up) for c in range(CHUNKS)
    ]
    send_down = [
        remote(bown.at[:, row_span(c)], gathered[1][c], y_send.at[1, c], y_recv.at[1, c], to_down) for c in range(CHUNKS)
    ]
    pass_on = [
        remote(gathered[0][c], gathered[2][c], y_send.at[2, c], y_recv.at[2, c], to_up)
        if c < half
        else remote(gathered[1][c], gathered[2][c], y_send.at[2, c], y_recv.at[2, c], to_down)
        for c in range(CHUNKS)
    ]
    up_order = list(range(CHUNKS))
    down_order = up_order[half:] + up_order[:half]
    for cu, cd in zip(up_order, down_order):
        send_up[cu].start()
        send_down[cd].start()

    @pl.when(has_r)
    def _():
        ids_r.start()

    @pl.when(has_l)
    def _():
        pl.semaphore_wait(entered, 1)
        ids_l.start()

    @pl.when(has_l)
    def _():
        ids_r.wait_recv()
        for q in range(2):
            ids[q] = lax.rem(got_l[1, 3 * q + 2], owned)

    @pl.when(jnp.logical_not(has_l))
    def _():
        for q in range(2):
            ids[q] = lax.rem(pairs[1, 3 * q], owned)

    @pl.when(has_r)
    def _():
        ids_l.wait_recv()
        for q in range(2):
            ids[2 + q] = lax.rem(got_r[1, 3 * q], owned)

    @pl.when(jnp.logical_not(has_r))
    def _():
        for q in range(2):
            ids[2 + q] = lax.rem(pairs[1, 3 * q + 2], owned)

    def halo_left(s, c):
        span = row_span(c)
        return remote(stage_l.at[s, :, span], halo_r.at[s, :, span], z_send.at[0, s, c], z_recv.at[0, s, c], to_l)

    def halo_right(s, c):
        span = row_span(c)
        return remote(stage_r.at[s, :, span], halo_l.at[s, :, span], z_send.at[1, s, c], z_recv.at[1, s, c], to_r)

    def pick(s, c, k):
        return bown[k, row_span(c), :] if s == 0 else gathered[s - 1][c][k]

    def stage(s, c):
        span = row_span(c)

        @pl.when(has_l)
        def _():
            for q in range(2):
                stage_l[s, q, span, :] = pick(s, c, ids[q])
            halo_left(s, c).start()

        @pl.when(jnp.logical_not(has_l))
        def _():
            for q in range(2):
                halo_l[s, q, span, :] = pick(s, c, ids[q])

        @pl.when(has_r)
        def _():
            for q in range(2):
                stage_r[s, q, span, :] = pick(s, c, ids[2 + q])
            halo_right(s, c).start()

        @pl.when(jnp.logical_not(has_r))
        def _():
            for q in range(2):
                halo_r[s, q, span, :] = pick(s, c, ids[2 + q])

    def wait_right(s):
        @pl.when(has_r)
        def _():
            for c in range(CHUNKS):
                halo_left(s, c).wait_recv()

    def wait_left(s):
        @pl.when(has_l)
        def _():
            for c in range(CHUNKS):
                halo_right(s, c).wait_recv()

    def own(s, k):
        return bown[k] if s == 0 else jnp.concatenate([g[k] for g in gathered[s - 1]], axis=0)

    def metric_rows(s):
        source = lax.rem(y + (0, 3, 1, 2)[s], 4)
        return m[pl.ds(pl.multiple_of(source * width, width), width), :]

    def put_c(s, slot, value):
        if s == 0:
            acc_c[slot] = value
        elif s < 3:
            acc_c[slot] += value
        else:
            cb[slot] = (acc_c[slot] + value).astype(BF16)

    def put_i(s, slot, value):
        if s == 0:
            acc_i[slot] = value
        elif s < 3:
            acc_i[slot] += value
        else:
            amp[slot] = ((acc_i[slot] + value) * recip[slot]).astype(BF16)

    def compute_own(s):
        @pl.loop(0, owned)
        def _(k):
            put_c(s, k, dot(own(s, k), metric_rows(s)))

        @pl.loop(0, 2)
        def _(q):
            p = 3 * q + 1
            put_i(s, p, dot_nt(own(s, lax.rem(pairs[0, p], owned)), own(s, lax.rem(pairs[1, p], owned))))

    def compute_left(s, q):
        put_i(s, 3 * q, dot_nt(own(s, lax.rem(pairs[0, 3 * q], owned)), halo_l[s, q]))

    def compute_right(s, q):
        put_i(s, 3 * q + 2, dot_nt(own(s, lax.rem(pairs[0, 3 * q + 2], owned)), halo_r[s, q]))

    def compute_left_c(s, q):
        put_c(s, owned + q, dot(halo_l[s, q], metric_rows(s)))

    def compute_right_c(s, q):
        put_c(s, owned + 2 + q, dot(halo_r[s, q], metric_rows(s)))

    def both_left(s):
        @pl.loop(0, 2)
        def _(q):
            compute_left(s, q)
            compute_left_c(s, q)

    def both_right(s):
        @pl.loop(0, 2)
        def _(q):
            compute_right(s, q)
            compute_right_c(s, q)

    for c in range(CHUNKS):
        stage(0, c)

    lanes = min(128, virt)
    load_occ.wait()
    load_vir.wait()
    vir_row = vir[...].reshape(1, virt)
    vir_rows = jnp.broadcast_to(vir_row, (lanes, virt))
    vir_cols = vir_rows.T

    @pl.loop(0, 6)
    def _(p):
        energy = occ[pairs[0, p]] + occ[pairs[1, p]]
        for t in range(virt // lanes):
            span = slice(t * lanes, (t + 1) * lanes)
            recip[p, :, span] = 1.0 / ((energy - vir_cols) - vir_row[:, span])

    load_m.wait()
    compute_own(0)

    for cu, cd in zip(up_order, down_order):
        send_up[cu].wait_recv()
        if cu < half:
            pass_on[cu].start()
        stage(1, cu)
        send_down[cd].wait_recv()
        if cd >= half:
            pass_on[cd].start()
        stage(2, cd)

    def stage_passed(c):
        for d in (c, half + c):
            pass_on[d].wait_recv()
            stage(3, d)

    compute_own(1)
    compute_own(2)
    for s in range(3):
        wait_right(s)
        both_right(s)
    wait_left(0)
    both_left(0)
    for c in range(half - 1):
        stage_passed(c)
    for s in (1, 2):
        wait_left(s)
        both_left(s)
    stage_passed(half - 1)
    compute_own(3)
    term_l = [remote(tsend_l.at[q], trecv_r.at[q], t_send.at[0, q], t_recv.at[0, q], to_l) for q in range(2)]
    term_r = [remote(tsend_r.at[q], trecv_l.at[q], t_send.at[1, q], t_recv.at[1, q], to_r) for q in range(2)]
    for ready, work, slot, has, copies, far, near in (
        (wait_right, compute_right, 2, has_r, term_r, tsend_r, trecv_r),
        (wait_left, compute_left, 0, has_l, term_l, tsend_l, trecv_l),
    ):
        ready(3)
        for q in range(2):
            p = 3 * q + slot
            work(3, q)
            value = dot_tn(amp[p], cb[lax.rem(pairs[0, p], owned)]).astype(BF16)

            @pl.when(has)
            def _():
                far[q] = value
                copies[q].start()

            @pl.when(jnp.logical_not(has))
            def _():
                near[q] = value

    @pl.loop(0, 2)
    def _(q):
        compute_left_c(3, q)
        compute_right_c(3, q)
        p = 3 * q
        term[p] = dot(amp[p], cb[owned + q])
        term[p + 1] = dot(amp[p + 1], cb[lax.rem(pairs[1, p + 1], owned)])
        term[p + 2] = dot(amp[p + 2], cb[owned + 2 + q])
        term[6 + q] = dot_tn(amp[p + 1], cb[lax.rem(pairs[0, p + 1], owned)])

    step = 16
    targets = [lax.rem(pairs[0, p], owned) for p in range(6)] + [lax.rem(pairs[1, 3 * q + 1], owned) for q in range(2)]

    @pl.loop(0, virt // step)
    def _(t):
        span = pl.ds(pl.multiple_of(t * step, step), step)
        values = [term[n, span, :] for n in range(8)]
        for k in range(owned):
            total[k, span, :] = sum(jnp.where(target == k, 1.0, 0.0) * v for target, v in zip(targets, values))

    for q in range(2):

        @pl.when(has_r)
        def _():
            term_l[q].wait_recv()

        @pl.when(has_l)
        def _():
            term_r[q].wait_recv()

    arrived = [ids[n] for n in range(4)]

    @pl.loop(0, virt // step)
    def _(t):
        span = pl.ds(pl.multiple_of(t * step, step), step)
        values = [trecv_l[q, span, :].astype(F32) for q in range(2)] + [trecv_r[q, span, :].astype(F32) for q in range(2)]
        for k in range(owned):
            more = sum(jnp.where(target == k, 1.0, 0.0) * v for target, v in zip(arrived, values))
            out[k, span, :] = (total[k, span, :] + more).astype(BF16)

    for c in range(CHUNKS):
        send_up[c].wait_send()
        send_down[c].wait_send()
        pass_on[c].wait_send()

    @pl.when(has_l)
    def _():
        ids_l.wait_send()
        for q in range(2):
            term_l[q].wait_send()
        for s in range(4):
            for c in range(CHUNKS):
                halo_left(s, c).wait_send()

    @pl.when(has_r)
    def _():
        ids_r.wait_send()
        for q in range(2):
            term_r[q].wait_send()
        for s in range(4):
            for c in range(CHUNKS):
                halo_right(s, c).wait_send()


def local(n_orb, b, metric, occ, vir, pairs):
    pairs_t = pairs.T
    owned, virt, width = b.shape
    rows = virt // CHUNKS
    vmem = pltpu.VMEM
    dma = pltpu.SemaphoreType.DMA
    scratch = [
        pltpu.SMEM(occ.shape, F32),
        vmem(vir.shape, F32),
        pltpu.SMEM(pairs_t.shape, jnp.int32),
        vmem((owned, virt, width), BF16),
        vmem(metric.shape, BF16),
        tuple(tuple(vmem((owned, rows, width), BF16) for _ in range(CHUNKS)) for _ in range(3)),
        vmem((4, 2, virt, width), BF16),
        vmem((4, 2, virt, width), BF16),
        vmem((4, 2, virt, width), BF16),
        vmem((4, 2, virt, width), BF16),
        pltpu.SMEM(pairs_t.shape, jnp.int32),
        pltpu.SMEM(pairs_t.shape, jnp.int32),
        pltpu.SMEM((4,), jnp.int32),
        vmem((6, virt, virt), F32),
        vmem((6, virt, virt), F32),
        vmem((owned + 4, virt, width), F32),
        vmem((owned + 4, virt, width), BF16),
        vmem((6, virt, virt), BF16),
        vmem((8, virt, width), F32),
        vmem((owned, virt, width), F32),
        vmem((2, virt, width), BF16),
        vmem((2, virt, width), BF16),
        vmem((2, virt, width), BF16),
        vmem((2, virt, width), BF16),
        dma((5,)),
        pltpu.SemaphoreType.REGULAR,
        dma((2,)),
        dma((2,)),
        dma((3, CHUNKS)),
        dma((3, CHUNKS)),
        dma((2, 4, CHUNKS)),
        dma((2, 4, CHUNKS)),
        dma((2, 2)),
        dma((2, 2)),
    ]
    return pl.pallas_call(
        functools.partial(kernel, n_orb),
        out_shape=jax.ShapeDtypeStruct(b.shape, BF16),
        in_specs=[pl.BlockSpec(memory_space=pltpu.HBM)] * 5,
        out_specs=pl.BlockSpec(memory_space=pltpu.VMEM),
        scratch_shapes=scratch,
        compiler_params=pltpu.CompilerParams(
            collective_id=0, has_side_effects=True, vmem_limit_bytes=52 * 2**20
        ),
    )(b, metric, occ, vir, pairs_t)


def solution(mesh):
    placed = (P("orb", None, "aux"), P(None, "aux"), P(), P(), P("orb", None))
    return jax.shard_map(
        functools.partial(local, mesh.shape["orb"]),
        mesh=mesh,
        in_specs=placed,
        out_specs=P("orb", None, "aux"),
        check_vma=False,
    )
```

```python
import functools

import jax
import jax.numpy as jnp
from jax import lax
from jax.experimental import pallas as pl
from jax.experimental.pallas import tpu as pltpu
from jax.sharding import PartitionSpec as P

MESH = pl.DeviceIdType.MESH
F32 = jnp.float32
BF16 = jnp.bfloat16
PARTS = (96, 64, 32)
LINE = 32


def dot(a, b):
    return lax.dot_general(a, b, (((1,), (0,)), ((), ())), preferred_element_type=F32)


def dot_nt(a, b):
    return lax.dot_general(a, b, (((1,), (1,)), ((), ())), preferred_element_type=F32)


def dot_tn(a, b):
    return lax.dot_general(a, b, (((0,), (0,)), ((), ())), preferred_element_type=F32)


def chunk_rows(virt):
    sizes = [part * virt // (2 * sum(PARTS)) for part in PARTS] * 2
    return sizes, [sum(sizes[:c]) for c in range(len(sizes))]


def kernel(
    n_orb,
    b_hbm,
    m_hbm,
    occ_hbm,
    vir_hbm,
    pairs_hbm,
    out,
    occ,
    vir,
    pairs,
    bown,
    m,
    gathered,
    halo_l,
    halo_r,
    stage_l,
    stage_r,
    got_l,
    got_r,
    ids,
    acc_i,
    recip,
    acc_c,
    cb,
    amp,
    term,
    total,
    tsend_l,
    tsend_r,
    trecv_l,
    trecv_r,
    load_sem,
    entered,
    id_send,
    id_recv,
    y_send,
    y_recv,
    z_send,
    z_recv,
    t_send,
    t_recv,
):
    owned, virt, width = bown.shape
    sizes, starts = chunk_rows(virt)
    count = len(sizes)
    half = count // 2
    o = lax.axis_index("orb")
    y = lax.axis_index("aux")
    has_l = o > 0
    has_r = o < n_orb - 1
    up, down = lax.rem(y + 1, 4), lax.rem(y + 3, 4)
    to_up, to_down = (o, up), (o, down)
    to_l, to_r = (o - 1, y), (o + 1, y)

    load_b = pltpu.make_async_copy(b_hbm, bown, load_sem.at[0])
    sources = (y, down, up, lax.rem(y + 2, 4))
    load_m = [
        pltpu.make_async_copy(
            m_hbm.at[pl.ds(pl.multiple_of(source * width, width), width), :],
            m.at[pl.ds(s * width, width), :],
            load_sem.at[4 + s],
        )
        for s, source in enumerate(sources)
    ]
    load_pairs = pltpu.make_async_copy(pairs_hbm, pairs, load_sem.at[1])
    load_occ = pltpu.make_async_copy(occ_hbm, occ, load_sem.at[2])
    load_vir = pltpu.make_async_copy(vir_hbm, vir, load_sem.at[3])
    load_pairs.start()
    load_b.start()
    load_occ.start()
    load_vir.start()
    for piece in load_m:
        piece.start()

    barrier = pltpu.get_barrier_semaphore()
    pl.semaphore_signal(barrier, inc=1, device_id=to_up, device_id_type=MESH)
    pl.semaphore_signal(barrier, inc=1, device_id=to_down, device_id_type=MESH)

    @pl.when(has_l)
    def _():
        pl.semaphore_signal(barrier, inc=1, device_id=to_l, device_id_type=MESH)

    pl.semaphore_wait(barrier, 2 + has_r.astype(jnp.int32))

    @pl.when(has_r)
    def _():
        pl.semaphore_signal(entered, inc=1, device_id=to_r, device_id_type=MESH)

    load_pairs.wait()
    load_b.wait()

    def remote(src, dst, send, recv, device):
        return pltpu.make_async_remote_copy(
            src_ref=src, dst_ref=dst, send_sem=send, recv_sem=recv, device_id=device, device_id_type=MESH
        )

    ids_l = remote(pairs, got_r, id_send.at[0], id_recv.at[0], to_l)
    ids_r = remote(pairs, got_l, id_send.at[1], id_recv.at[1], to_r)

    def row_span(c):
        return pl.ds(starts[c], sizes[c])

    send_up = [
        remote(bown.at[:, row_span(c)], gathered[0][c], y_send.at[0, c], y_recv.at[0, c], to_up) for c in range(count)
    ]
    send_down = [
        remote(bown.at[:, row_span(c)], gathered[1][c], y_send.at[1, c], y_recv.at[1, c], to_down) for c in range(count)
    ]
    pass_on = [
        remote(gathered[0][c], gathered[2][c], y_send.at[2, c], y_recv.at[2, c], to_up)
        if c < half
        else remote(gathered[1][c], gathered[2][c], y_send.at[2, c], y_recv.at[2, c], to_down)
        for c in range(count)
    ]
    up_order = list(range(count))
    down_order = up_order[half:] + up_order[:half]
    for cu, cd in zip(up_order, down_order):
        send_up[cu].start()
        send_down[cd].start()

    @pl.when(has_r)
    def _():
        ids_r.start()

    @pl.when(has_l)
    def _():
        pl.semaphore_wait(entered, 1)
        ids_l.start()

    @pl.when(has_l)
    def _():
        ids_r.wait_recv()
        for q in range(2):
            ids[q] = lax.rem(got_l[1, 3 * q + 2], owned)

    @pl.when(jnp.logical_not(has_l))
    def _():
        for q in range(2):
            ids[q] = lax.rem(pairs[1, 3 * q], owned)

    @pl.when(has_r)
    def _():
        ids_l.wait_recv()
        for q in range(2):
            ids[2 + q] = lax.rem(got_r[1, 3 * q], owned)

    @pl.when(jnp.logical_not(has_r))
    def _():
        for q in range(2):
            ids[2 + q] = lax.rem(pairs[1, 3 * q + 2], owned)

    def lanes_of(s):
        return pl.ds(s * width, width)

    def halo_left(s, c):
        span = row_span(c)
        return remote(stage_l.at[s, :, span], halo_r.at[:, span, lanes_of(s)], z_send.at[0, s, c], z_recv.at[0, s, c], to_l)

    def halo_right(s, c):
        span = row_span(c)
        return remote(stage_r.at[s, :, span], halo_l.at[:, span, lanes_of(s)], z_send.at[1, s, c], z_recv.at[1, s, c], to_r)

    def pick(s, c, k):
        return bown[k, row_span(c), :] if s == 0 else gathered[s - 1][c][k]

    def stage(s, c):
        span = row_span(c)

        @pl.when(has_l)
        def _():
            for q in range(2):
                stage_l[s, q, span, :] = pick(s, c, ids[q])
            halo_left(s, c).start()

        @pl.when(jnp.logical_not(has_l))
        def _():
            for q in range(2):
                halo_l[q, span, lanes_of(s)] = pick(s, c, ids[q])

        @pl.when(has_r)
        def _():
            for q in range(2):
                stage_r[s, q, span, :] = pick(s, c, ids[2 + q])
            halo_right(s, c).start()

        @pl.when(jnp.logical_not(has_r))
        def _():
            for q in range(2):
                halo_r[q, span, lanes_of(s)] = pick(s, c, ids[2 + q])

    def wait_right(s):
        @pl.when(has_r)
        def _():
            for c in range(count):
                halo_left(s, c).wait_recv()

    def wait_left(s):
        @pl.when(has_l)
        def _():
            for c in range(count):
                halo_right(s, c).wait_recv()

    def own(lo, hi, k):
        parts = [
            bown[k] if s == 0 else jnp.concatenate([g[k] for g in gathered[s - 1]], axis=0) for s in range(lo, hi)
        ]
        return parts[0] if len(parts) == 1 else jnp.concatenate(parts, axis=1)

    def metric_rows(lo, hi):
        return m[pl.ds(lo * width, (hi - lo) * width), :]

    def halo(ref, lo, hi, q):
        return ref[q, :, pl.ds(lo * width, (hi - lo) * width)]

    def put_c(lo, hi, slot, value):
        if hi == 4:
            cb[slot] = (acc_c[slot] + value).astype(BF16)
        elif lo == 0:
            acc_c[slot] = value
        else:
            acc_c[slot] += value

    def put_i(lo, hi, slot, value):
        if hi == 4:
            amp[slot] = ((acc_i[slot] + value) * recip[slot]).astype(BF16)
        elif lo == 0:
            acc_i[slot] = value
        else:
            acc_i[slot] += value

    def compute_own_c(lo, hi):
        @pl.loop(0, owned)
        def _(k):
            put_c(lo, hi, k, dot(own(lo, hi, k), metric_rows(lo, hi)))

    def compute_own_i(lo, hi):
        @pl.loop(0, 2)
        def _(q):
            p = 3 * q + 1
            first = own(lo, hi, lax.rem(pairs[0, p], owned))
            put_i(lo, hi, p, dot_nt(first, own(lo, hi, lax.rem(pairs[1, p], owned))))

    def compute_left(lo, hi, q):
        first = own(lo, hi, lax.rem(pairs[0, 3 * q], owned))
        put_i(lo, hi, 3 * q, dot_nt(first, halo(halo_l, lo, hi, q)))

    def compute_right(lo, hi, q):
        first = own(lo, hi, lax.rem(pairs[0, 3 * q + 2], owned))
        put_i(lo, hi, 3 * q + 2, dot_nt(first, halo(halo_r, lo, hi, q)))

    def compute_left_c(lo, hi, q):
        put_c(lo, hi, owned + q, dot(halo(halo_l, lo, hi, q), metric_rows(lo, hi)))

    def compute_right_c(lo, hi, q):
        put_c(lo, hi, owned + 2 + q, dot(halo(halo_r, lo, hi, q), metric_rows(lo, hi)))

    def both_left(lo, hi):
        @pl.loop(0, 2)
        def _(q):
            compute_left(lo, hi, q)
            compute_left_c(lo, hi, q)

    def both_right(lo, hi):
        @pl.loop(0, 2)
        def _(q):
            compute_right(lo, hi, q)
            compute_right_c(lo, hi, q)

    for c in range(count):
        stage(0, c)

    lanes = min(128, virt)
    load_occ.wait()
    load_vir.wait()
    vir_row = vir[...].reshape(1, virt)
    vir_rows = jnp.broadcast_to(vir_row, (lanes, virt))
    vir_cols = vir_rows.T

    @pl.loop(0, 6)
    def _(p):
        energy = occ[pairs[0, p]] + occ[pairs[1, p]]
        for t in range(virt // lanes):
            span = slice(t * lanes, (t + 1) * lanes)
            recip[p, :, span] = 1.0 / ((energy - vir_cols) - vir_row[:, span])

    for piece in load_m:
        piece.wait()
    compute_own_c(0, 1)
    compute_own_i(0, 1)

    for cu, cd in zip(up_order, down_order):
        send_up[cu].wait_recv()
        if cu < half:
            pass_on[cu].start()
        stage(1, cu)
        send_down[cd].wait_recv()
        if cd >= half:
            pass_on[cd].start()
        stage(2, cd)

    def stage_passed(c):
        for d in (c, half + c):
            pass_on[d].wait_recv()
            stage(3, d)

    compute_own_c(1, 3)
    compute_own_i(1, 3)
    for s in range(3):
        wait_right(s)
    both_right(0, 3)
    for c in range(half - 1):
        stage_passed(c)
    for s in range(3):
        wait_left(s)
    both_left(0, 3)
    stage_passed(half - 1)

    term_l = [remote(tsend_l.at[q], trecv_r.at[q], t_send.at[0, q], t_recv.at[0, q], to_l) for q in range(2)]
    term_r = [remote(tsend_r.at[q], trecv_l.at[q], t_send.at[1, q], t_recv.at[1, q], to_r) for q in range(2)]
    sides = (
        (wait_left, compute_left, 0, has_l, term_l, tsend_l, trecv_l),
        (wait_right, compute_right, 2, has_r, term_r, tsend_r, trecv_r),
    )

    def give_terms(side):
        ready, work, slot, has, copies, far, near = sides[side]
        ready(3)
        for q in range(2):
            p = 3 * q + slot
            work(3, 4, q)
            value = dot_tn(amp[p], cb[lax.rem(pairs[0, p], owned)]).astype(BF16)

            @pl.when(has)
            def _():
                far[q] = value
                copies[q].start()

            @pl.when(jnp.logical_not(has))
            def _():
                near[q] = value

    def keep_terms(side):
        @pl.loop(0, 2)
        def _(q):
            (compute_left_c, compute_right_c)[side](3, 4, q)
            p = 3 * q + 2 * side
            term[p] = dot(amp[p], cb[owned + 2 * side + q])

    step = 16

    def gather_terms(terms, start, finish):
        @pl.loop(0, virt // step)
        def _(t):
            span = pl.ds(pl.multiple_of(t * step, step), step)
            values = [ref[n, span, :].astype(F32) for ref, n, _ in terms]
            for k in range(owned):
                more = sum(jnp.where(target == k, 1.0, 0.0) * v for (_, _, target), v in zip(terms, values))
                if not start:
                    more += total[k, span, :]
                if finish:
                    out[k, span, :] = more.astype(BF16)
                else:
                    total[k, span, :] = more

    early_right = jnp.logical_and(has_r, lax.rem(o, LINE) == LINE - 1)
    late_left = jnp.logical_and(has_l, lax.rem(o, LINE) == 0)

    compute_own_c(3, 4)

    @pl.when(early_right)
    def _():
        give_terms(1)

    compute_own_i(3, 4)

    @pl.when(jnp.logical_not(early_right))
    def _():
        give_terms(1)

    left_of = [lax.rem(pairs[0, p], owned) for p in range(6)]

    def own_terms():
        @pl.loop(0, 2)
        def _(q):
            p = 3 * q + 1
            term[p] = dot(amp[p], cb[lax.rem(pairs[1, p], owned)])
            term[6 + q] = dot_tn(amp[p], cb[lax.rem(pairs[0, p], owned)])

        gather_terms(
            [(term, 1, left_of[1]), (term, 4, left_of[4])]
            + [(term, 6 + q, lax.rem(pairs[1, 3 * q + 1], owned)) for q in range(2)],
            True,
            False,
        )

    @pl.when(late_left)
    def _():
        own_terms()
        keep_terms(1)

    give_terms(0)

    @pl.when(jnp.logical_not(late_left))
    def _():
        own_terms()
        keep_terms(1)

    keep_terms(0)

    for q in range(2):

        @pl.when(has_r)
        def _():
            term_l[q].wait_recv()

        @pl.when(has_l)
        def _():
            term_r[q].wait_recv()

        kept = [(term, p, left_of[p]) for p in (0, 2, 3, 5)] if q == 0 else []
        gather_terms(kept + [(trecv_l, q, ids[q]), (trecv_r, q, ids[2 + q])], False, q == 1)

    for c in range(count):
        send_up[c].wait_send()
        send_down[c].wait_send()
        pass_on[c].wait_send()

    @pl.when(has_l)
    def _():
        ids_l.wait_send()
        for q in range(2):
            term_l[q].wait_send()
        for s in range(4):
            for c in range(count):
                halo_left(s, c).wait_send()

    @pl.when(has_r)
    def _():
        ids_r.wait_send()
        for q in range(2):
            term_r[q].wait_send()
        for s in range(4):
            for c in range(count):
                halo_right(s, c).wait_send()


def local(n_orb, b, metric, occ, vir, pairs):
    pairs_t = pairs.T
    owned, virt, width = b.shape
    sizes, _ = chunk_rows(virt)
    count = len(sizes)
    vmem = pltpu.VMEM
    dma = pltpu.SemaphoreType.DMA
    scratch = [
        pltpu.SMEM(occ.shape, F32),
        vmem(vir.shape, F32),
        pltpu.SMEM(pairs_t.shape, jnp.int32),
        vmem((owned, virt, width), BF16),
        vmem(metric.shape, BF16),
        tuple(tuple(vmem((owned, rows, width), BF16) for rows in sizes) for _ in range(3)),
        vmem((2, virt, 4 * width), BF16),
        vmem((2, virt, 4 * width), BF16),
        vmem((4, 2, virt, width), BF16),
        vmem((4, 2, virt, width), BF16),
        pltpu.SMEM(pairs_t.shape, jnp.int32),
        pltpu.SMEM(pairs_t.shape, jnp.int32),
        pltpu.SMEM((4,), jnp.int32),
        vmem((6, virt, virt), F32),
        vmem((6, virt, virt), F32),
        vmem((owned + 4, virt, width), F32),
        vmem((owned + 4, virt, width), BF16),
        vmem((6, virt, virt), BF16),
        vmem((8, virt, width), F32),
        vmem((owned, virt, width), F32),
        vmem((2, virt, width), BF16),
        vmem((2, virt, width), BF16),
        vmem((2, virt, width), BF16),
        vmem((2, virt, width), BF16),
        dma((8,)),
        pltpu.SemaphoreType.REGULAR,
        dma((2,)),
        dma((2,)),
        dma((3, count)),
        dma((3, count)),
        dma((2, 4, count)),
        dma((2, 4, count)),
        dma((2, 2)),
        dma((2, 2)),
    ]
    return pl.pallas_call(
        functools.partial(kernel, n_orb),
        out_shape=jax.ShapeDtypeStruct(b.shape, BF16),
        in_specs=[pl.BlockSpec(memory_space=pltpu.HBM)] * 5,
        out_specs=pl.BlockSpec(memory_space=pltpu.VMEM),
        scratch_shapes=scratch,
        compiler_params=pltpu.CompilerParams(
            collective_id=0, has_side_effects=True, vmem_limit_bytes=52 * 2**20
        ),
    )(b, metric, *(pltpu.with_memory_space_constraint(a, pltpu.HBM) for a in (occ, vir, pairs_t)))


def solution(mesh):
    placed = (P("orb", None, "aux"), P(None, "aux"), P(), P(), P("orb", None))
    return jax.shard_map(
        functools.partial(local, mesh.shape["orb"]),
        mesh=mesh,
        in_specs=placed,
        out_specs=P("orb", None, "aux"),
        check_vma=False,
    )
```

```python
import functools

import jax
import jax.numpy as jnp
from jax import lax
from jax.experimental import pallas as pl
from jax.experimental.pallas import tpu as pltpu
from jax.sharding import PartitionSpec as P

MESH = pl.DeviceIdType.MESH
F32 = jnp.float32
BF16 = jnp.bfloat16
PARTS = (96, 64, 32)
LINE = 32


def dot(a, b):
    return lax.dot_general(a, b, (((1,), (0,)), ((), ())), preferred_element_type=F32)


def dot_nt(a, b):
    return lax.dot_general(a, b, (((1,), (1,)), ((), ())), preferred_element_type=F32)


def dot_tn(a, b):
    return lax.dot_general(a, b, (((0,), (0,)), ((), ())), preferred_element_type=F32)


def chunk_rows(virt):
    sizes = [part * virt // (2 * sum(PARTS)) for part in PARTS] * 2
    return sizes, [sum(sizes[:c]) for c in range(len(sizes))]


def kernel(
    n_orb,
    b_hbm,
    m_hbm,
    occ_hbm,
    vir_hbm,
    pairs_hbm,
    out,
    occ,
    vir,
    pairs,
    bown,
    m,
    gathered,
    halo_l,
    halo_r,
    stage_l,
    stage_r,
    got_l,
    got_r,
    ids,
    acc_i,
    recip,
    acc_c,
    cb,
    amp,
    term,
    total,
    tsend_l,
    tsend_r,
    trecv_l,
    trecv_r,
    load_sem,
    entered,
    id_send,
    id_recv,
    y_send,
    y_recv,
    z_send,
    z_recv,
    t_send,
    t_recv,
):
    owned, virt, width = bown.shape
    sizes, starts = chunk_rows(virt)
    count = len(sizes)
    half = count // 2
    o = lax.axis_index("orb")
    y = lax.axis_index("aux")
    has_l = o > 0
    has_r = o < n_orb - 1
    up, down = lax.rem(y + 1, 4), lax.rem(y + 3, 4)
    to_up, to_down = (o, up), (o, down)
    to_l, to_r = (o - 1, y), (o + 1, y)

    load_b = pltpu.make_async_copy(b_hbm, bown, load_sem.at[0])
    sources = (y, down, up, lax.rem(y + 2, 4))
    load_m = [
        pltpu.make_async_copy(
            m_hbm.at[pl.ds(pl.multiple_of(source * width, width), width), :],
            m.at[pl.ds(s * width, width), :],
            load_sem.at[4 + s],
        )
        for s, source in enumerate(sources)
    ]
    load_pairs = pltpu.make_async_copy(pairs_hbm, pairs, load_sem.at[1])
    load_occ = pltpu.make_async_copy(occ_hbm, occ, load_sem.at[2])
    load_vir = pltpu.make_async_copy(vir_hbm, vir, load_sem.at[3])
    load_pairs.start()
    load_b.start()
    load_occ.start()
    load_vir.start()
    for piece in load_m:
        piece.start()

    barrier = pltpu.get_barrier_semaphore()
    pl.semaphore_signal(barrier, inc=1, device_id=to_up, device_id_type=MESH)
    pl.semaphore_signal(barrier, inc=1, device_id=to_down, device_id_type=MESH)

    @pl.when(has_l)
    def _():
        pl.semaphore_signal(barrier, inc=1, device_id=to_l, device_id_type=MESH)

    pl.semaphore_wait(barrier, 2 + has_r.astype(jnp.int32))

    @pl.when(has_r)
    def _():
        pl.semaphore_signal(entered, inc=1, device_id=to_r, device_id_type=MESH)

    load_pairs.wait()
    load_b.wait()

    def remote(src, dst, send, recv, device):
        return pltpu.make_async_remote_copy(
            src_ref=src, dst_ref=dst, send_sem=send, recv_sem=recv, device_id=device, device_id_type=MESH
        )

    ids_l = remote(pairs, got_r, id_send.at[0], id_recv.at[0], to_l)
    ids_r = remote(pairs, got_l, id_send.at[1], id_recv.at[1], to_r)

    def row_span(c):
        return pl.ds(starts[c], sizes[c])

    send_up = [
        remote(bown.at[:, row_span(c)], gathered[0][c], y_send.at[0, c], y_recv.at[0, c], to_up) for c in range(count)
    ]
    send_down = [
        remote(bown.at[:, row_span(c)], gathered[1][c], y_send.at[1, c], y_recv.at[1, c], to_down) for c in range(count)
    ]
    pass_on = [
        remote(gathered[0][c], gathered[2][c], y_send.at[2, c], y_recv.at[2, c], to_up)
        if c < half
        else remote(gathered[1][c], gathered[2][c], y_send.at[2, c], y_recv.at[2, c], to_down)
        for c in range(count)
    ]
    up_order = list(range(count))
    down_order = up_order[half:] + up_order[:half]

    def start_ring():
        for cu, cd in zip(up_order, down_order):
            send_up[cu].start()
            send_down[cd].start()

    yields = lax.rem(o, LINE) == LINE - 2

    @pl.when(jnp.logical_not(yields))
    def _():
        start_ring()

    @pl.when(has_r)
    def _():
        ids_r.start()

    @pl.when(has_l)
    def _():
        pl.semaphore_wait(entered, 1)
        ids_l.start()

    @pl.when(has_l)
    def _():
        ids_r.wait_recv()
        for q in range(2):
            ids[q] = lax.rem(got_l[1, 3 * q + 2], owned)

    @pl.when(jnp.logical_not(has_l))
    def _():
        for q in range(2):
            ids[q] = lax.rem(pairs[1, 3 * q], owned)

    @pl.when(has_r)
    def _():
        ids_l.wait_recv()
        for q in range(2):
            ids[2 + q] = lax.rem(got_r[1, 3 * q], owned)

    @pl.when(jnp.logical_not(has_r))
    def _():
        for q in range(2):
            ids[2 + q] = lax.rem(pairs[1, 3 * q + 2], owned)

    def lanes_of(s):
        return pl.ds(s * width, width)

    def halo_left(s, c):
        span = row_span(c)
        return remote(stage_l.at[s, :, span], halo_r.at[:, span, lanes_of(s)], z_send.at[0, s, c], z_recv.at[0, s, c], to_l)

    def halo_right(s, c):
        span = row_span(c)
        return remote(stage_r.at[s, :, span], halo_l.at[:, span, lanes_of(s)], z_send.at[1, s, c], z_recv.at[1, s, c], to_r)

    def pick(s, c, k):
        return bown[k, row_span(c), :] if s == 0 else gathered[s - 1][c][k]

    def stage(s, c):
        span = row_span(c)

        @pl.when(has_l)
        def _():
            for q in range(2):
                stage_l[s, q, span, :] = pick(s, c, ids[q])
            halo_left(s, c).start()

        @pl.when(jnp.logical_not(has_l))
        def _():
            for q in range(2):
                halo_l[q, span, lanes_of(s)] = pick(s, c, ids[q])

        @pl.when(has_r)
        def _():
            for q in range(2):
                stage_r[s, q, span, :] = pick(s, c, ids[2 + q])
            halo_right(s, c).start()

        @pl.when(jnp.logical_not(has_r))
        def _():
            for q in range(2):
                halo_r[q, span, lanes_of(s)] = pick(s, c, ids[2 + q])

    def wait_right(s):
        @pl.when(has_r)
        def _():
            for c in range(count):
                halo_left(s, c).wait_recv()

    def wait_left(s):
        @pl.when(has_l)
        def _():
            for c in range(count):
                halo_right(s, c).wait_recv()

    def own(lo, hi, k):
        parts = [
            bown[k] if s == 0 else jnp.concatenate([g[k] for g in gathered[s - 1]], axis=0) for s in range(lo, hi)
        ]
        return parts[0] if len(parts) == 1 else jnp.concatenate(parts, axis=1)

    def metric_rows(lo, hi):
        return m[pl.ds(lo * width, (hi - lo) * width), :]

    def halo(ref, lo, hi, q):
        return ref[q, :, pl.ds(lo * width, (hi - lo) * width)]

    def put_c(lo, hi, slot, value):
        if hi == 4:
            cb[slot] = (acc_c[slot] + value).astype(BF16)
        elif lo == 0:
            acc_c[slot] = value
        else:
            acc_c[slot] += value

    def put_i(lo, hi, slot, value):
        if hi == 4:
            amp[slot] = ((acc_i[slot] + value) * recip[slot]).astype(BF16)
        elif lo == 0:
            acc_i[slot] = value
        else:
            acc_i[slot] += value

    def compute_own_c(lo, hi):
        @pl.loop(0, owned)
        def _(k):
            put_c(lo, hi, k, dot(own(lo, hi, k), metric_rows(lo, hi)))

    def compute_own_i(lo, hi):
        @pl.loop(0, 2)
        def _(q):
            p = 3 * q + 1
            first = own(lo, hi, lax.rem(pairs[0, p], owned))
            put_i(lo, hi, p, dot_nt(first, own(lo, hi, lax.rem(pairs[1, p], owned))))

    def compute_left(lo, hi, q):
        first = own(lo, hi, lax.rem(pairs[0, 3 * q], owned))
        put_i(lo, hi, 3 * q, dot_nt(first, halo(halo_l, lo, hi, q)))

    def compute_right(lo, hi, q):
        first = own(lo, hi, lax.rem(pairs[0, 3 * q + 2], owned))
        put_i(lo, hi, 3 * q + 2, dot_nt(first, halo(halo_r, lo, hi, q)))

    def compute_left_c(lo, hi, q):
        put_c(lo, hi, owned + q, dot(halo(halo_l, lo, hi, q), metric_rows(lo, hi)))

    def compute_right_c(lo, hi, q):
        put_c(lo, hi, owned + 2 + q, dot(halo(halo_r, lo, hi, q), metric_rows(lo, hi)))

    def both_left(lo, hi):
        @pl.loop(0, 2)
        def _(q):
            compute_left(lo, hi, q)
            compute_left_c(lo, hi, q)

    def both_right(lo, hi):
        @pl.loop(0, 2)
        def _(q):
            compute_right(lo, hi, q)
            compute_right_c(lo, hi, q)

    for c in range(count):
        stage(0, c)

    lanes = min(128, virt)
    load_occ.wait()
    load_vir.wait()
    vir_row = vir[...].reshape(1, virt)
    vir_rows = jnp.broadcast_to(vir_row, (lanes, virt))
    vir_cols = vir_rows.T

    @pl.loop(0, 6)
    def _(p):
        energy = occ[pairs[0, p]] + occ[pairs[1, p]]
        for t in range(virt // lanes):
            span = slice(t * lanes, (t + 1) * lanes)
            recip[p, :, span] = 1.0 / ((energy - vir_cols) - vir_row[:, span])

    for piece in load_m:
        piece.wait()
    compute_own_c(0, 1)
    compute_own_i(0, 1)

    @pl.when(yields)
    def _():
        start_ring()

    for cu, cd in zip(up_order, down_order):
        send_up[cu].wait_recv()
        if cu < half:
            pass_on[cu].start()
        stage(1, cu)
        send_down[cd].wait_recv()
        if cd >= half:
            pass_on[cd].start()
        stage(2, cd)

    def stage_passed(c):
        for d in (c, half + c):
            pass_on[d].wait_recv()
            stage(3, d)

    compute_own_c(1, 3)
    compute_own_i(1, 3)
    for s in range(3):
        wait_right(s)
    both_right(0, 3)
    for c in range(half - 1):
        stage_passed(c)
    for s in range(3):
        wait_left(s)
    both_left(0, 3)
    stage_passed(half - 1)

    term_l = [remote(tsend_l.at[q], trecv_r.at[q], t_send.at[0, q], t_recv.at[0, q], to_l) for q in range(2)]
    term_r = [remote(tsend_r.at[q], trecv_l.at[q], t_send.at[1, q], t_recv.at[1, q], to_r) for q in range(2)]
    sides = (
        (wait_left, compute_left, 0, has_l, term_l, tsend_l, trecv_l),
        (wait_right, compute_right, 2, has_r, term_r, tsend_r, trecv_r),
    )

    def give_terms(side):
        ready, work, slot, has, copies, far, near = sides[side]
        ready(3)
        for q in range(2):
            p = 3 * q + slot
            work(3, 4, q)
            value = dot_tn(amp[p], cb[lax.rem(pairs[0, p], owned)]).astype(BF16)

            @pl.when(has)
            def _():
                far[q] = value
                copies[q].start()

            @pl.when(jnp.logical_not(has))
            def _():
                near[q] = value

    def keep_terms(side):
        @pl.loop(0, 2)
        def _(q):
            (compute_left_c, compute_right_c)[side](3, 4, q)
            p = 3 * q + 2 * side
            term[p] = dot(amp[p], cb[owned + 2 * side + q])

    step = 16

    def gather_terms(terms, start, finish):
        @pl.loop(0, virt // step)
        def _(t):
            span = pl.ds(pl.multiple_of(t * step, step), step)
            values = [ref[n, span, :].astype(F32) for ref, n, _ in terms]
            for k in range(owned):
                more = sum(jnp.where(target == k, 1.0, 0.0) * v for (_, _, target), v in zip(terms, values))
                if not start:
                    more += total[k, span, :]
                if finish:
                    out[k, span, :] = more.astype(BF16)
                else:
                    total[k, span, :] = more

    early_right = jnp.logical_and(has_r, lax.rem(o, LINE) == LINE - 1)
    late_left = jnp.logical_and(has_l, lax.rem(o, LINE) == 0)

    compute_own_c(3, 4)

    @pl.when(early_right)
    def _():
        give_terms(1)

    compute_own_i(3, 4)

    @pl.when(jnp.logical_not(early_right))
    def _():
        give_terms(1)

    left_of = [lax.rem(pairs[0, p], owned) for p in range(6)]

    def own_terms():
        @pl.loop(0, 2)
        def _(q):
            p = 3 * q + 1
            term[p] = dot(amp[p], cb[lax.rem(pairs[1, p], owned)])
            term[6 + q] = dot_tn(amp[p], cb[lax.rem(pairs[0, p], owned)])

        gather_terms(
            [(term, 1, left_of[1]), (term, 4, left_of[4])]
            + [(term, 6 + q, lax.rem(pairs[1, 3 * q + 1], owned)) for q in range(2)],
            True,
            False,
        )

    @pl.when(late_left)
    def _():
        own_terms()
        keep_terms(1)

    give_terms(0)

    @pl.when(jnp.logical_not(late_left))
    def _():
        own_terms()
        keep_terms(1)

    keep_terms(0)

    for q in range(2):

        @pl.when(has_r)
        def _():
            term_l[q].wait_recv()

        @pl.when(has_l)
        def _():
            term_r[q].wait_recv()

        kept = [(term, p, left_of[p]) for p in (0, 2, 3, 5)] if q == 0 else []
        gather_terms(kept + [(trecv_l, q, ids[q]), (trecv_r, q, ids[2 + q])], False, q == 1)

    for c in range(count):
        send_up[c].wait_send()
        send_down[c].wait_send()
        pass_on[c].wait_send()

    @pl.when(has_l)
    def _():
        ids_l.wait_send()
        for q in range(2):
            term_l[q].wait_send()
        for s in range(4):
            for c in range(count):
                halo_left(s, c).wait_send()

    @pl.when(has_r)
    def _():
        ids_r.wait_send()
        for q in range(2):
            term_r[q].wait_send()
        for s in range(4):
            for c in range(count):
                halo_right(s, c).wait_send()


def local(n_orb, b, metric, occ, vir, pairs):
    pairs_t = pairs.T
    owned, virt, width = b.shape
    sizes, _ = chunk_rows(virt)
    count = len(sizes)
    vmem = pltpu.VMEM
    dma = pltpu.SemaphoreType.DMA
    scratch = [
        pltpu.SMEM(occ.shape, F32),
        vmem(vir.shape, F32),
        pltpu.SMEM(pairs_t.shape, jnp.int32),
        vmem((owned, virt, width), BF16),
        vmem(metric.shape, BF16),
        tuple(tuple(vmem((owned, rows, width), BF16) for rows in sizes) for _ in range(3)),
        vmem((2, virt, 4 * width), BF16),
        vmem((2, virt, 4 * width), BF16),
        vmem((4, 2, virt, width), BF16),
        vmem((4, 2, virt, width), BF16),
        pltpu.SMEM(pairs_t.shape, jnp.int32),
        pltpu.SMEM(pairs_t.shape, jnp.int32),
        pltpu.SMEM((4,), jnp.int32),
        vmem((6, virt, virt), F32),
        vmem((6, virt, virt), F32),
        vmem((owned + 4, virt, width), F32),
        vmem((owned + 4, virt, width), BF16),
        vmem((6, virt, virt), BF16),
        vmem((8, virt, width), F32),
        vmem((owned, virt, width), F32),
        vmem((2, virt, width), BF16),
        vmem((2, virt, width), BF16),
        vmem((2, virt, width), BF16),
        vmem((2, virt, width), BF16),
        dma((8,)),
        pltpu.SemaphoreType.REGULAR,
        dma((2,)),
        dma((2,)),
        dma((3, count)),
        dma((3, count)),
        dma((2, 4, count)),
        dma((2, 4, count)),
        dma((2, 2)),
        dma((2, 2)),
    ]
    return pl.pallas_call(
        functools.partial(kernel, n_orb),
        out_shape=jax.ShapeDtypeStruct(b.shape, BF16),
        in_specs=[pl.BlockSpec(memory_space=pltpu.HBM)] * 5,
        out_specs=pl.BlockSpec(memory_space=pltpu.VMEM),
        scratch_shapes=scratch,
        compiler_params=pltpu.CompilerParams(
            collective_id=0, has_side_effects=True, vmem_limit_bytes=52 * 2**20
        ),
    )(b, metric, *(pltpu.with_memory_space_constraint(a, pltpu.HBM) for a in (occ, vir, pairs_t)))


def solution(mesh):
    placed = (P("orb", None, "aux"), P(None, "aux"), P(), P(), P("orb", None))
    return jax.shard_map(
        functools.partial(local, mesh.shape["orb"]),
        mesh=mesh,
        in_specs=placed,
        out_specs=P("orb", None, "aux"),
        check_vma=False,
    )
```

```python
import functools

import jax
import jax.numpy as jnp
from jax import lax
from jax.experimental import pallas as pl
from jax.experimental.pallas import tpu as pltpu
from jax.sharding import PartitionSpec as P

MESH = pl.DeviceIdType.MESH
F32 = jnp.float32
BF16 = jnp.bfloat16
PARTS = (96, 64, 32)
LINE = 32


def dot(a, b):
    return lax.dot_general(a, b, (((1,), (0,)), ((), ())), preferred_element_type=F32)


def dot_nt(a, b):
    return lax.dot_general(a, b, (((1,), (1,)), ((), ())), preferred_element_type=F32)


def dot_tn(a, b):
    return lax.dot_general(a, b, (((0,), (0,)), ((), ())), preferred_element_type=F32)


def chunk_rows(virt):
    sizes = [part * virt // (2 * sum(PARTS)) for part in PARTS] * 2
    return sizes, [sum(sizes[:c]) for c in range(len(sizes))]


def kernel(
    n_orb,
    b_hbm,
    m_hbm,
    occ_hbm,
    vir_hbm,
    pairs_hbm,
    out,
    occ,
    vir,
    pairs,
    bown,
    m,
    gathered,
    halo_l,
    halo_r,
    stage_l,
    stage_r,
    got_l,
    got_r,
    ids,
    acc_i,
    recip,
    acc_c,
    cb,
    amp,
    term,
    total,
    tsend_l,
    tsend_r,
    trecv_l,
    trecv_r,
    load_sem,
    entered,
    id_send,
    id_recv,
    y_send,
    y_recv,
    z_send,
    z_recv,
    t_send,
    t_recv,
):
    owned, virt, width = bown.shape
    sizes, starts = chunk_rows(virt)
    count = len(sizes)
    half = count // 2
    o = lax.axis_index("orb")
    y = lax.axis_index("aux")
    has_l = o > 0
    has_r = o < n_orb - 1
    up, down = lax.rem(y + 1, 4), lax.rem(y + 3, 4)
    to_up, to_down = (o, up), (o, down)
    to_l, to_r = (o - 1, y), (o + 1, y)

    load_b = pltpu.make_async_copy(b_hbm, bown, load_sem.at[0])
    sources = (y, down, up, lax.rem(y + 2, 4))
    load_m = [
        pltpu.make_async_copy(
            m_hbm.at[pl.ds(pl.multiple_of(source * width, width), width), :],
            m.at[pl.ds(s * width, width), :],
            load_sem.at[4 + s],
        )
        for s, source in enumerate(sources)
    ]
    load_pairs = pltpu.make_async_copy(pairs_hbm, pairs, load_sem.at[1])
    load_occ = pltpu.make_async_copy(occ_hbm, occ, load_sem.at[2])
    load_vir = pltpu.make_async_copy(vir_hbm, vir, load_sem.at[3])
    load_pairs.start()
    load_b.start()
    load_occ.start()
    load_vir.start()
    for piece in load_m:
        piece.start()

    barrier = pltpu.get_barrier_semaphore()
    pl.semaphore_signal(barrier, inc=1, device_id=to_up, device_id_type=MESH)
    pl.semaphore_signal(barrier, inc=1, device_id=to_down, device_id_type=MESH)

    @pl.when(has_l)
    def _():
        pl.semaphore_signal(barrier, inc=1, device_id=to_l, device_id_type=MESH)

    pl.semaphore_wait(barrier, 2 + has_r.astype(jnp.int32))

    @pl.when(has_r)
    def _():
        pl.semaphore_signal(entered, inc=1, device_id=to_r, device_id_type=MESH)

    load_pairs.wait()
    load_b.wait()

    def remote(src, dst, send, recv, device):
        return pltpu.make_async_remote_copy(
            src_ref=src, dst_ref=dst, send_sem=send, recv_sem=recv, device_id=device, device_id_type=MESH
        )

    ids_l = remote(pairs, got_r, id_send.at[0], id_recv.at[0], to_l)
    ids_r = remote(pairs, got_l, id_send.at[1], id_recv.at[1], to_r)

    def row_span(c):
        return pl.ds(starts[c], sizes[c])

    send_up = [
        remote(bown.at[:, row_span(c)], gathered[0][c], y_send.at[0, c], y_recv.at[0, c], to_up) for c in range(count)
    ]
    send_down = [
        remote(bown.at[:, row_span(c)], gathered[1][c], y_send.at[1, c], y_recv.at[1, c], to_down) for c in range(count)
    ]
    pass_on = [
        remote(gathered[0][c], gathered[2][c], y_send.at[2, c], y_recv.at[2, c], to_up)
        if c < half
        else remote(gathered[1][c], gathered[2][c], y_send.at[2, c], y_recv.at[2, c], to_down)
        for c in range(count)
    ]
    up_order = list(range(count))
    down_order = up_order[half:] + up_order[:half]

    def start_ring():
        for cu, cd in zip(up_order, down_order):
            send_up[cu].start()
            send_down[cd].start()

    place = lax.rem(o, LINE)
    yields = jnp.logical_or(place == LINE - 2, jnp.logical_or(place == 9, place == 17))

    @pl.when(jnp.logical_not(yields))
    def _():
        start_ring()

    @pl.when(has_r)
    def _():
        ids_r.start()

    @pl.when(has_l)
    def _():
        pl.semaphore_wait(entered, 1)
        ids_l.start()

    @pl.when(has_l)
    def _():
        ids_r.wait_recv()
        for q in range(2):
            ids[q] = lax.rem(got_l[1, 3 * q + 2], owned)

    @pl.when(jnp.logical_not(has_l))
    def _():
        for q in range(2):
            ids[q] = lax.rem(pairs[1, 3 * q], owned)

    @pl.when(has_r)
    def _():
        ids_l.wait_recv()
        for q in range(2):
            ids[2 + q] = lax.rem(got_r[1, 3 * q], owned)

    @pl.when(jnp.logical_not(has_r))
    def _():
        for q in range(2):
            ids[2 + q] = lax.rem(pairs[1, 3 * q + 2], owned)

    def lanes_of(s):
        return pl.ds(s * width, width)

    def halo_left(s, c):
        span = row_span(c)
        return remote(stage_l.at[s, :, span], halo_r.at[:, span, lanes_of(s)], z_send.at[0, s, c], z_recv.at[0, s, c], to_l)

    def halo_right(s, c):
        span = row_span(c)
        return remote(stage_r.at[s, :, span], halo_l.at[:, span, lanes_of(s)], z_send.at[1, s, c], z_recv.at[1, s, c], to_r)

    def pick(s, c, k):
        return bown[k, row_span(c), :] if s == 0 else gathered[s - 1][c][k]

    def stage(s, c):
        span = row_span(c)

        @pl.when(has_l)
        def _():
            for q in range(2):
                stage_l[s, q, span, :] = pick(s, c, ids[q])
            halo_left(s, c).start()

        @pl.when(jnp.logical_not(has_l))
        def _():
            for q in range(2):
                halo_l[q, span, lanes_of(s)] = pick(s, c, ids[q])

        @pl.when(has_r)
        def _():
            for q in range(2):
                stage_r[s, q, span, :] = pick(s, c, ids[2 + q])
            halo_right(s, c).start()

        @pl.when(jnp.logical_not(has_r))
        def _():
            for q in range(2):
                halo_r[q, span, lanes_of(s)] = pick(s, c, ids[2 + q])

    def wait_right(s):
        @pl.when(has_r)
        def _():
            for c in range(count):
                halo_left(s, c).wait_recv()

    def wait_left(s):
        @pl.when(has_l)
        def _():
            for c in range(count):
                halo_right(s, c).wait_recv()

    def own(lo, hi, k):
        parts = [
            bown[k] if s == 0 else jnp.concatenate([g[k] for g in gathered[s - 1]], axis=0) for s in range(lo, hi)
        ]
        return parts[0] if len(parts) == 1 else jnp.concatenate(parts, axis=1)

    def metric_rows(lo, hi):
        return m[pl.ds(lo * width, (hi - lo) * width), :]

    def halo(ref, lo, hi, q):
        return ref[q, :, pl.ds(lo * width, (hi - lo) * width)]

    def put_c(lo, hi, slot, value):
        if hi == 4:
            cb[slot] = (acc_c[slot] + value).astype(BF16)
        elif lo == 0:
            acc_c[slot] = value
        else:
            acc_c[slot] += value

    def put_i(lo, hi, slot, value):
        if hi == 4:
            amp[slot] = ((acc_i[slot] + value) * recip[slot]).astype(BF16)
        elif lo == 0:
            acc_i[slot] = value
        else:
            acc_i[slot] += value

    def compute_own_c(lo, hi):
        @pl.loop(0, owned)
        def _(k):
            put_c(lo, hi, k, dot(own(lo, hi, k), metric_rows(lo, hi)))

    def compute_own_i(lo, hi):
        @pl.loop(0, 2)
        def _(q):
            p = 3 * q + 1
            first = own(lo, hi, lax.rem(pairs[0, p], owned))
            put_i(lo, hi, p, dot_nt(first, own(lo, hi, lax.rem(pairs[1, p], owned))))

    def compute_left(lo, hi, q):
        first = own(lo, hi, lax.rem(pairs[0, 3 * q], owned))
        put_i(lo, hi, 3 * q, dot_nt(first, halo(halo_l, lo, hi, q)))

    def compute_right(lo, hi, q):
        first = own(lo, hi, lax.rem(pairs[0, 3 * q + 2], owned))
        put_i(lo, hi, 3 * q + 2, dot_nt(first, halo(halo_r, lo, hi, q)))

    def compute_left_c(lo, hi, q):
        put_c(lo, hi, owned + q, dot(halo(halo_l, lo, hi, q), metric_rows(lo, hi)))

    def compute_right_c(lo, hi, q):
        put_c(lo, hi, owned + 2 + q, dot(halo(halo_r, lo, hi, q), metric_rows(lo, hi)))

    def both_left(lo, hi):
        @pl.loop(0, 2)
        def _(q):
            compute_left(lo, hi, q)
            compute_left_c(lo, hi, q)

    def both_right(lo, hi):
        @pl.loop(0, 2)
        def _(q):
            compute_right(lo, hi, q)
            compute_right_c(lo, hi, q)

    for c in range(count):
        stage(0, c)

    lanes = min(128, virt)
    load_occ.wait()
    load_vir.wait()
    vir_row = vir[...].reshape(1, virt)
    vir_rows = jnp.broadcast_to(vir_row, (lanes, virt))
    vir_cols = vir_rows.T

    @pl.loop(0, 6)
    def _(p):
        energy = occ[pairs[0, p]] + occ[pairs[1, p]]
        for t in range(virt // lanes):
            span = slice(t * lanes, (t + 1) * lanes)
            recip[p, :, span] = 1.0 / ((energy - vir_cols) - vir_row[:, span])

    for piece in load_m:
        piece.wait()
    compute_own_c(0, 1)

    @pl.when(yields)
    def _():
        start_ring()

    compute_own_i(0, 1)

    for cu, cd in zip(up_order, down_order):
        send_up[cu].wait_recv()
        if cu < half:
            pass_on[cu].start()
        stage(1, cu)
        send_down[cd].wait_recv()
        if cd >= half:
            pass_on[cd].start()
        stage(2, cd)

    def stage_passed(c):
        for d in (c, half + c):
            pass_on[d].wait_recv()
            stage(3, d)

    compute_own_c(1, 3)
    compute_own_i(1, 3)
    for s in range(3):
        wait_right(s)
    both_right(0, 3)
    for c in range(half - 1):
        stage_passed(c)
    for s in range(3):
        wait_left(s)
    both_left(0, 3)
    stage_passed(half - 1)

    term_l = [remote(tsend_l.at[q], trecv_r.at[q], t_send.at[0, q], t_recv.at[0, q], to_l) for q in range(2)]
    term_r = [remote(tsend_r.at[q], trecv_l.at[q], t_send.at[1, q], t_recv.at[1, q], to_r) for q in range(2)]
    sides = (
        (wait_left, compute_left, 0, has_l, term_l, tsend_l, trecv_l),
        (wait_right, compute_right, 2, has_r, term_r, tsend_r, trecv_r),
    )

    def give_terms(side):
        ready, work, slot, has, copies, far, near = sides[side]
        ready(3)
        for q in range(2):
            p = 3 * q + slot
            work(3, 4, q)
            value = dot_tn(amp[p], cb[lax.rem(pairs[0, p], owned)]).astype(BF16)

            @pl.when(has)
            def _():
                far[q] = value
                copies[q].start()

            @pl.when(jnp.logical_not(has))
            def _():
                near[q] = value

    def keep_terms(side):
        @pl.loop(0, 2)
        def _(q):
            (compute_left_c, compute_right_c)[side](3, 4, q)
            p = 3 * q + 2 * side
            term[p] = dot(amp[p], cb[owned + 2 * side + q])

    step = 16

    def gather_terms(terms, start, finish):
        @pl.loop(0, virt // step)
        def _(t):
            span = pl.ds(pl.multiple_of(t * step, step), step)
            values = [ref[n, span, :].astype(F32) for ref, n, _ in terms]
            for k in range(owned):
                more = sum(jnp.where(target == k, 1.0, 0.0) * v for (_, _, target), v in zip(terms, values))
                if not start:
                    more += total[k, span, :]
                if finish:
                    out[k, span, :] = more.astype(BF16)
                else:
                    total[k, span, :] = more

    early_right = jnp.logical_and(has_r, lax.rem(o, LINE) == LINE - 1)
    late_left = jnp.logical_and(has_l, lax.rem(o, LINE) == 0)

    compute_own_c(3, 4)

    @pl.when(early_right)
    def _():
        give_terms(1)

    compute_own_i(3, 4)

    @pl.when(jnp.logical_not(early_right))
    def _():
        give_terms(1)

    left_of = [lax.rem(pairs[0, p], owned) for p in range(6)]

    def own_terms():
        @pl.loop(0, 2)
        def _(q):
            p = 3 * q + 1
            term[p] = dot(amp[p], cb[lax.rem(pairs[1, p], owned)])
            term[6 + q] = dot_tn(amp[p], cb[lax.rem(pairs[0, p], owned)])

        gather_terms(
            [(term, 1, left_of[1]), (term, 4, left_of[4])]
            + [(term, 6 + q, lax.rem(pairs[1, 3 * q + 1], owned)) for q in range(2)],
            True,
            False,
        )

    @pl.when(late_left)
    def _():
        own_terms()
        keep_terms(1)

    give_terms(0)

    @pl.when(jnp.logical_not(late_left))
    def _():
        own_terms()
        keep_terms(1)

    keep_terms(0)

    for q in range(2):

        @pl.when(has_r)
        def _():
            term_l[q].wait_recv()

        @pl.when(has_l)
        def _():
            term_r[q].wait_recv()

        kept = [(term, p, left_of[p]) for p in (0, 2, 3, 5)] if q == 0 else []
        gather_terms(kept + [(trecv_l, q, ids[q]), (trecv_r, q, ids[2 + q])], False, q == 1)

    for c in range(count):
        send_up[c].wait_send()
        send_down[c].wait_send()
        pass_on[c].wait_send()

    @pl.when(has_l)
    def _():
        ids_l.wait_send()
        for q in range(2):
            term_l[q].wait_send()
        for s in range(4):
            for c in range(count):
                halo_left(s, c).wait_send()

    @pl.when(has_r)
    def _():
        ids_r.wait_send()
        for q in range(2):
            term_r[q].wait_send()
        for s in range(4):
            for c in range(count):
                halo_right(s, c).wait_send()


def local(n_orb, b, metric, occ, vir, pairs):
    pairs_t = pairs.T
    owned, virt, width = b.shape
    sizes, _ = chunk_rows(virt)
    count = len(sizes)
    vmem = pltpu.VMEM
    dma = pltpu.SemaphoreType.DMA
    scratch = [
        pltpu.SMEM(occ.shape, F32),
        vmem(vir.shape, F32),
        pltpu.SMEM(pairs_t.shape, jnp.int32),
        vmem((owned, virt, width), BF16),
        vmem(metric.shape, BF16),
        tuple(tuple(vmem((owned, rows, width), BF16) for rows in sizes) for _ in range(3)),
        vmem((2, virt, 4 * width), BF16),
        vmem((2, virt, 4 * width), BF16),
        vmem((4, 2, virt, width), BF16),
        vmem((4, 2, virt, width), BF16),
        pltpu.SMEM(pairs_t.shape, jnp.int32),
        pltpu.SMEM(pairs_t.shape, jnp.int32),
        pltpu.SMEM((4,), jnp.int32),
        vmem((6, virt, virt), F32),
        vmem((6, virt, virt), F32),
        vmem((owned + 4, virt, width), F32),
        vmem((owned + 4, virt, width), BF16),
        vmem((6, virt, virt), BF16),
        vmem((8, virt, width), F32),
        vmem((owned, virt, width), F32),
        vmem((2, virt, width), BF16),
        vmem((2, virt, width), BF16),
        vmem((2, virt, width), BF16),
        vmem((2, virt, width), BF16),
        dma((8,)),
        pltpu.SemaphoreType.REGULAR,
        dma((2,)),
        dma((2,)),
        dma((3, count)),
        dma((3, count)),
        dma((2, 4, count)),
        dma((2, 4, count)),
        dma((2, 2)),
        dma((2, 2)),
    ]
    return pl.pallas_call(
        functools.partial(kernel, n_orb),
        out_shape=jax.ShapeDtypeStruct(b.shape, BF16),
        in_specs=[pl.BlockSpec(memory_space=pltpu.HBM)] * 5,
        out_specs=pl.BlockSpec(memory_space=pltpu.VMEM),
        scratch_shapes=scratch,
        compiler_params=pltpu.CompilerParams(
            collective_id=0, has_side_effects=True, vmem_limit_bytes=52 * 2**20
        ),
    )(b, metric, *(pltpu.with_memory_space_constraint(a, pltpu.HBM) for a in (occ, vir, pairs_t)))


def solution(mesh):
    placed = (P("orb", None, "aux"), P(None, "aux"), P(), P(), P("orb", None))
    return jax.shard_map(
        functools.partial(local, mesh.shape["orb"]),
        mesh=mesh,
        in_specs=placed,
        out_specs=P("orb", None, "aux"),
        check_vma=False,
    )
```
